32 devices in a mesh: fsdp: 8 (over z, y), ctx: 2 (over core), tp: 2 (over x).
Axes of the slice: x: 2, y: 2, z: 4, core: 2. Of those that a mesh axis runs over, the one named last changes fastest.
Arguments:
- image: float32 [8, 56, 56, 512], P('fsdp', 'ctx', 'tp'), may hold values from -6 to 6
- cotangent: float32 [8, 56, 56, 512], P('fsdp', 'ctx', 'tp'), may hold values from -6 to 6
- norm_gain: bfloat16 [2, 512], P(None, ('fsdp', 'ctx')), may hold values from 0.25 to 1.75
- norm_bias: bfloat16 [2, 512], P(None, ('fsdp', 'ctx')), may hold values from -1.75 to 1.75
- qkv_weight: bfloat16 [512, 3, 512], P(('fsdp', 'ctx'), None, 'tp'), may hold values from -2 to 2
- qkv_bias: bfloat16 [2, 512], P(None, 'tp'), may hold values from -3 to 3
- bias_table: bfloat16 [16, 169], P('tp'), may hold values from -6 to 6
- bias_index: int32 [49, 49], replicated, may hold values from 0 to 168
- regions: int32 [56, 56], P('ctx'), may hold values from 0 to 8, as said below
- proj_weight: bfloat16 [512, 512], P('tp', ('fsdp', 'ctx')), may hold values from -1 to 1
- out_bias: bfloat16 [2, 512], P(None, ('fsdp', 'ctx')), may hold values from -1.75 to 1.75
- up_weight: bfloat16 [512, 2048], P(('fsdp', 'ctx'), 'tp'), may hold values from -0.25 to 0.25
- up_bias: bfloat16 [2048], P('tp'), may hold values from -3 to 3
- down_weight: bfloat16 [2048, 512], P('tp', ('fsdp', 'ctx')), may hold values from -0.1875 to 0.1875
Outputs:
- output: float32 [8, 56, 56, 512], P('fsdp', 'ctx', 'tp')
- image_grad: float32 [8, 56, 56, 512], P('fsdp', 'ctx', 'tp')
- norm_gain_grad: float32 [2, 512], P(None, ('fsdp', 'ctx'))
- norm_bias_grad: float32 [2, 512], P(None, ('fsdp', 'ctx'))
- qkv_weight_grad: float32 [512, 3, 512], P(('fsdp', 'ctx'), None, 'tp')
- qkv_bias_grad: float32 [2, 512], P(None, 'tp')
- bias_table_grad: float32 [16, 169], P('tp')
- proj_weight_grad: float32 [512, 512], P('tp', ('fsdp', 'ctx'))
- out_bias_grad: float32 [2, 512], P(None, ('fsdp', 'ctx'))
- up_weight_grad: float32 [512, 2048], P(('fsdp', 'ctx'), 'tp')
- up_bias_grad: float32 [2048], P('tp')
- down_weight_grad: float32 [2048, 512], P('tp', ('fsdp', 'ctx'))
The draws below stay inside these ranges and needn't reach their ends.
Inputs may be any that keep to these rules, and one draw needn't show every extreme that they name: `bias_index`: for each query position and key position of a window, the row of bias_table that holds their bias. `regions`: 3 times a row label plus a column label; each label counts how many of two boundaries near the end of the grid the row or column has passed.
All inputs are finite; a program needn't handle non-finite values.
Results may differ from the reference program's by a relative error of at most 0.015.
Values may be sent and summed in bfloat16 or wider, within the bound.
A program may use at most 192 MiB of HBM per device.

```python
import math
import jax
import jax.numpy as jnp
from jax import lax

DIM = 512
HEADS = 16
HEAD_DIM = 32
FFN = 2048
WIN = 7
SHIFT = 3
SIDE = 56
IMAGES = 8
TABLE = 169
N_TP = 2


def draw_qkv_weight(key, part):
    drawn = jnp.clip(jax.random.normal(key, (DIM, 3, DIM), jnp.float32), -4.0, 4.0) * (1.0 / math.sqrt(DIM))
    return jnp.clip(drawn, -2.0, 2.0).astype(jnp.bfloat16)


def band_labels(key):
    split_keys = jax.random.split(key, 2)
    outer_edge = jax.random.randint(split_keys[0], (), WIN - 2, WIN + 3)
    inner_edge = jax.random.randint(split_keys[1], (), 1, outer_edge)
    line_index = jnp.arange(SIDE, dtype=jnp.int32)
    return (line_index >= SIDE - outer_edge).astype(jnp.int32) + (line_index >= SIDE - inner_edge).astype(jnp.int32)


def draw_regions(key, part):
    split_keys = jax.random.split(jax.random.fold_in(key, 17), 2)
    row_labels = band_labels(split_keys[0])
    col_labels = band_labels(split_keys[1])
    return 3 * row_labels[:, None] + col_labels[None, :]


def plant(entries, own_key, smallest, top_value):
    dims = entries.shape
    spot = [jax.random.randint(jax.random.fold_in(own_key, axis), (), 0, dims[axis]) for axis in range(len(dims))]
    entries = entries.at[tuple(spot)].set(smallest)
    longest = dims.index(max(dims))
    spot[longest] = (spot[longest] + 1) % dims[longest]
    return entries.at[tuple(spot)].set(top_value)


def with_spikes(result, key, source, target, parts, factor):
    owner, partner = [(jnp.arange(result.shape[dim]) // (result.shape[dim] // parts)).reshape([-1 if axis == dim else 1 for axis in range(result.ndim)]) for dim in (source, target)]
    chosen = jax.random.permutation(key, parts)[partner]
    strong = (owner == chosen) | (owner == (partner + parts // 2) % parts)
    return jnp.where(strong, factor * result, result)


def levels(key, dims, cuts, least, high):
    gain = 1.0
    for position, parts in cuts:
        steps = jax.random.uniform(jax.random.fold_in(jax.random.fold_in(key, 6), position), (parts,), jnp.float32, least / len(cuts), high / len(cuts))
        gain = gain * jnp.repeat(jnp.exp(steps), dims[position] // parts).reshape((-1,) + (1,) * (len(dims) - 1 - position))
    return gain


def scatter_about(stream_key, shape, deviation, reach, cuts=(), kind=jnp.bfloat16):
    factor_of = levels(stream_key, shape, cuts, -0.22, 0.18) if cuts else 1.0
    values = jax.random.normal(stream_key, shape, jnp.float32) * deviation * factor_of
    return jnp.minimum(jnp.maximum(values, -reach), reach).astype(kind)


def heavy_noise(own_key, extent, deviation, most, shards, heavy, kind=jnp.bfloat16):
    values = deviation * jax.random.normal(own_key, extent, jnp.float32)
    if shards:
        values = values * levels(own_key, extent, shards, -0.22, 0.18)
    return jnp.clip(with_spikes(values, jax.random.fold_in(own_key, 3), *heavy), -most, most).astype(kind)


def setup_inputs(seed: int = 0) -> dict:
    splits = jax.random.split(jax.random.key(seed), 15)
    return {
        "image": heavy_noise(splits[0], (IMAGES, SIDE, SIDE, DIM), 1.0, 6.0, ((0, 8), (1, 2), (2, 2)), (0, 3, 8, 2.0), jnp.float32),
        "cotangent": heavy_noise(splits[1], (IMAGES, SIDE, SIDE, DIM), 1.0, 6.0, ((0, 8), (1, 2), (2, 2)), (0, 3, 8, 2.0), jnp.float32),
        "norm_gain": jnp.clip(1.0 + 0.15 * jax.random.normal(splits[2], (2, DIM), jnp.float32), 0.25, 1.75).astype(jnp.bfloat16),
        "norm_bias": scatter_about(splits[3], (2, DIM), 0.3, 1.75, ((1, 16),)),
        "qkv_weight": draw_qkv_weight(jax.random.fold_in(splits[14], 71), 0),
        "qkv_bias": scatter_about(splits[5], (2, DIM), 0.5, 3.0, ((1, 2),)),
        "bias_table": scatter_about(splits[6], (HEADS, TABLE), 1.0, 6.0, ((0, 2),)),
        "bias_index": plant(jax.random.randint(splits[7], (WIN * WIN, WIN * WIN), 0, TABLE), jax.random.fold_in(splits[7], 1), 0, TABLE - 1).astype(jnp.int32),
        "regions": draw_regions(jax.random.fold_in(splits[14], 71), 0),
        "proj_weight": scatter_about(splits[9], (DIM, DIM), (DIM // 16) ** -0.5, 1.0, ((0, 2), (1, 16))),
        "out_bias": scatter_about(splits[10], (2, DIM), 0.3, 1.75, ((1, 16),)),
        "up_weight": scatter_about(splits[11], (DIM, FFN), DIM ** -0.5, 0.25, ((0, 16), (1, 2))),
        "up_bias": scatter_about(splits[12], (FFN,), 0.5, 3.0, ((0, 2),)),
        "down_weight": scatter_about(splits[13], (FFN, DIM), (FFN // 2) ** -0.5, 0.1875, ((0, 2), (1, 16))),
    }


EPSILON = 1e-05
MASKED = -100.0

def layer_stats(values_in):
    mean_row = lax.optimization_barrier(jnp.mean(values_in, axis=-1, keepdims=True))
    centered = values_in - mean_row
    inverse = lax.rsqrt(lax.optimization_barrier(jnp.mean(centered * centered, axis=-1, keepdims=True)) + EPSILON)
    return (centered * inverse, inverse)

def layer_back(grad_out, normed, inverse, gain_row):
    scaled = grad_out * gain_row
    return inverse * (scaled - lax.optimization_barrier(jnp.mean(scaled, axis=-1, keepdims=True)) - normed * lax.optimization_barrier(jnp.mean(scaled * normed, axis=-1, keepdims=True)))

def gelu_exact(pre_act):
    return 0.5 * pre_act * (1.0 + lax.erf(pre_act * (1.0 / math.sqrt(2.0))))

def gelu_slope(pre_act):
    return 0.5 * (1.0 + lax.erf(pre_act * (1.0 / math.sqrt(2.0)))) + pre_act * jnp.exp(-0.5 * pre_act * pre_act) * (1.0 / math.sqrt(2.0 * math.pi))

def as_wide(narrow):
    return lax.optimization_barrier(narrow).astype(jnp.float32)

def grouped_sum(left_in, right_in, groups):
    width = left_in.shape[1] // groups
    running = jnp.zeros((left_in.shape[0], right_in.shape[1]), jnp.float32)
    for group_index in range(groups):
        piece = jnp.dot(left_in[:, group_index * width:(group_index + 1) * width], right_in[group_index * width:(group_index + 1) * width], preferred_element_type=jnp.float32)
        running = running + as_wide(piece.astype(jnp.bfloat16))
    return running

def reference(image, cotangent, norm_gain, norm_bias, qkv_weight, qkv_bias, bias_table, bias_index, regions, proj_weight, out_bias, up_weight, up_bias, down_weight):
    side_win = SIDE // WIN
    win_area = WIN * WIN
    score_scale = 1.0 / math.sqrt(HEAD_DIM)
    head_group = DIM // N_TP
    qkv_flat = qkv_weight.reshape(DIM, 3 * DIM)
    qkv_back = qkv_weight.reshape(DIM, 3, N_TP, head_group).transpose(2, 1, 3, 0).reshape(3 * DIM, DIM)
    rel_bias = bias_table.astype(jnp.float32)[:, bias_index]
    labels = regions.reshape(side_win, WIN, side_win, WIN).transpose(0, 2, 1, 3).reshape(side_win, side_win, win_area)
    mask_bias = jnp.where(labels[:, :, :, None] == labels[:, :, None, :], 0.0, MASKED).astype(jnp.float32)
    shape_five = (side_win, side_win, win_area, HEADS, HEAD_DIM)
    highest = lax.Precision.HIGHEST

    def windows(field_in):
        return field_in.reshape(side_win, WIN, side_win, WIN, -1).transpose(0, 2, 1, 3, 4).reshape(-1, field_in.shape[-1])

    def unwindows(tile_rows):
        return tile_rows.reshape(side_win, side_win, WIN, WIN, -1).transpose(0, 2, 1, 3, 4).reshape(SIDE, SIDE, -1)

    def one_image(totals, pair):
        block_in, grad_top = pair
        norm_one, inv_one = layer_stats(block_in)
        normed_one = (norm_one * norm_gain[0] + norm_bias[0]).astype(jnp.bfloat16)
        tokens = windows(jnp.roll(normed_one, (-SHIFT, -SHIFT), (0, 1)))
        mixed_all = jnp.dot(tokens, qkv_flat, preferred_element_type=jnp.float32).reshape(-1, 3, DIM)
        queries = (mixed_all[:, 0] + qkv_bias[0]).astype(jnp.bfloat16)
        keys_all = mixed_all[:, 1].astype(jnp.bfloat16)
        values_all = (mixed_all[:, 2] + qkv_bias[1]).astype(jnp.bfloat16)
        query_five = as_wide(queries).reshape(shape_five)
        key_five = as_wide(keys_all).reshape(shape_five)
        value_five = as_wide(values_all).reshape(shape_five)
        scores = jnp.einsum('abqhd,abkhd->abhqk', query_five, key_five, precision=highest) * score_scale + rel_bias + mask_bias[:, :, None]
        row_peak = lax.optimization_barrier(jnp.max(scores, axis=-1, keepdims=True))
        exp_scores = jnp.exp(scores - row_peak)
        row_total = lax.optimization_barrier(jnp.sum(exp_scores, axis=-1, keepdims=True))
        log_total = row_peak + jnp.log(row_total)
        prob_half = as_wide((exp_scores / row_total).astype(jnp.bfloat16))
        attended = jnp.einsum('abhqk,abkhd->abqhd', prob_half, value_five, precision=highest).astype(jnp.bfloat16).reshape(-1, DIM)
        attn_out = grouped_sum(attended, proj_weight, N_TP) + out_bias[0]
        middle = block_in + jnp.roll(unwindows(attn_out), (SHIFT, SHIFT), (0, 1))
        norm_two, inv_two = layer_stats(middle)
        normed_two = (norm_two * norm_gain[1] + norm_bias[1]).astype(jnp.bfloat16)
        rows_two = normed_two.reshape(-1, DIM)
        pre_act = jnp.dot(rows_two, up_weight, preferred_element_type=jnp.float32) + up_bias
        hidden = gelu_exact(pre_act).astype(jnp.bfloat16)
        output = middle + grouped_sum(hidden, down_weight, N_TP).reshape(SIDE, SIDE, DIM) + out_bias[1]
        grad_half = grad_top.reshape(-1, DIM).astype(jnp.bfloat16)
        grad_down = jnp.dot(hidden.T, grad_half, preferred_element_type=jnp.float32)
        slope_all = jnp.dot(grad_half, down_weight.T, preferred_element_type=jnp.float32) * gelu_slope(pre_act)
        slope_half = slope_all.astype(jnp.bfloat16)
        grad_up_bias = lax.optimization_barrier(jnp.sum(slope_all, axis=0))
        grad_up = jnp.dot(rows_two.T, slope_half, preferred_element_type=jnp.float32)
        grad_two = grouped_sum(slope_half, up_weight.T, N_TP).reshape(SIDE, SIDE, DIM)
        grad_middle = grad_top + layer_back(grad_two, norm_two, inv_two, norm_gain[1])
        grad_tokens = windows(jnp.roll(grad_middle, (-SHIFT, -SHIFT), (0, 1))).astype(jnp.bfloat16)
        grad_proj = jnp.dot(attended.T, grad_tokens, preferred_element_type=jnp.float32)
        grad_attended = jnp.dot(grad_tokens, proj_weight.T, preferred_element_type=jnp.float32).astype(jnp.bfloat16)
        grad_att_five = as_wide(grad_attended).reshape(shape_five)
        prob_row = jnp.exp(scores - log_total)
        grad_prob = jnp.einsum('abqhd,abkhd->abhqk', grad_att_five, value_five, precision=highest)
        grad_value = jnp.einsum('abhqk,abqhd->abkhd', as_wide(prob_row.astype(jnp.bfloat16)), grad_att_five, precision=highest)
        grad_score = prob_row * (grad_prob - lax.optimization_barrier(jnp.sum(prob_row * grad_prob, axis=-1, keepdims=True)))
        score_total = lax.optimization_barrier(jnp.sum(grad_score, axis=(0, 1))).reshape(HEADS, -1)
        grad_table = jax.ops.segment_sum(score_total.T, bias_index.reshape(-1), TABLE).T
        grad_score_half = as_wide((grad_score * score_scale).astype(jnp.bfloat16))
        grad_query = jnp.einsum('abhqk,abkhd->abqhd', grad_score_half, key_five, precision=highest).reshape(-1, DIM)
        grad_key = jnp.einsum('abhqk,abqhd->abkhd', grad_score_half, query_five, precision=highest).reshape(-1, DIM)
        grad_value = grad_value.reshape(-1, DIM)
        grad_qkv_bias = jnp.stack([lax.optimization_barrier(jnp.sum(grad_query, axis=0)), lax.optimization_barrier(jnp.sum(grad_value, axis=0))])
        grad_mixed = jnp.stack([grad_query, grad_key, grad_value], axis=1).astype(jnp.bfloat16)
        grad_qkv = jnp.dot(tokens.T, grad_mixed.reshape(-1, 3 * DIM), preferred_element_type=jnp.float32)
        grad_grouped = grad_mixed.reshape(-1, 3, N_TP, head_group).transpose(0, 2, 1, 3).reshape(-1, 3 * DIM)
        grad_one = jnp.roll(unwindows(grouped_sum(grad_grouped, qkv_back, N_TP)), (SHIFT, SHIFT), (0, 1))
        grad_start = grad_middle + layer_back(grad_one, norm_one, inv_one, norm_gain[0])
        sum_axes = (0, 1)
        gain_terms = jnp.stack([lax.optimization_barrier(jnp.sum(grad_one * norm_one, sum_axes)), lax.optimization_barrier(jnp.sum(grad_two * norm_two, sum_axes))])
        bias_terms = jnp.stack([lax.optimization_barrier(jnp.sum(grad_one, sum_axes)), lax.optimization_barrier(jnp.sum(grad_two, sum_axes))])
        out_terms = jnp.stack([lax.optimization_barrier(jnp.sum(grad_middle, sum_axes)), lax.optimization_barrier(jnp.sum(grad_top, sum_axes))])
        adds = (gain_terms, bias_terms, grad_qkv, grad_qkv_bias, grad_table, grad_proj, out_terms, grad_up, grad_up_bias, grad_down)
        totals = tuple((total + extra for total, extra in zip(totals, adds)))
        return (totals, (output, grad_start))
    zeros_init = (jnp.zeros((2, DIM), jnp.float32), jnp.zeros((2, DIM), jnp.float32), jnp.zeros((DIM, 3 * DIM), jnp.float32), jnp.zeros((2, DIM), jnp.float32), jnp.zeros((HEADS, TABLE), jnp.float32), jnp.zeros((DIM, DIM), jnp.float32), jnp.zeros((2, DIM), jnp.float32), jnp.zeros((DIM, FFN), jnp.float32), jnp.zeros((FFN,), jnp.float32), jnp.zeros((FFN, DIM), jnp.float32))
    totals, stacked = lax.scan(one_image, zeros_init, (image, cotangent))
    output, image_grad = stacked
    gain_grad, bias_grad, qkv_grad, qkv_bias_grad, table_grad, proj_grad, out_grad, up_grad, up_bias_grad, down_grad = totals
    return (output, image_grad, gain_grad, bias_grad, qkv_grad.reshape(DIM, 3, DIM), qkv_bias_grad, table_grad, proj_grad, out_grad, up_grad, up_bias_grad, down_grad)
```

```python
import math

import jax
import jax.numpy as jnp
from jax import lax
from jax.experimental import pallas as pl
from jax.experimental.pallas import tpu as pltpu
from jax.sharding import PartitionSpec as P

HEAD_DIM = 32
WIN = 7
PAD = 8
AREA = PAD * PAD
SHIFT = 3
GROUP = 8
LANES = GROUP * HEAD_DIM
TALL = GROUP * AREA
PER_STEP = 4
ROWS = PER_STEP * AREA

EPSILON = 1e-05
MASKED = -100.0
ABSENT = -1e30
SCALE = 1.0 / math.sqrt(HEAD_DIM)
F32 = jnp.float32
BF16 = jnp.bfloat16


def shifted(value, axis, steps):
    count = lax.axis_size(axis)
    pairs = [(source, (source + steps) % count) for source in range(count)]
    return lax.ppermute(value, axis, pairs)


def bits(axis):
    return [1 << k for k in range(lax.axis_size(axis).bit_length() - 1)]


def swap(value, axis, bit):
    return lax.ppermute(value, axis, [(i, i ^ bit) for i in range(lax.axis_size(axis))])


def own_bit(axis, bit):
    return (lax.axis_index(axis) // bit) % 2


def gather_blocks(block, tp_first):
    lead, rows, cols = block.shape
    place = 1
    held = block
    high_first = bits("fsdp")[::-1]
    keep_last = len(high_first) // 3
    early, late = high_first[: len(high_first) - keep_last], high_first[len(high_first) - keep_last :]
    tp_stages = [("tp", bit) for bit in bits("tp")]
    order = [("fsdp", bit) for bit in early]
    late_stages = [("fsdp", bit) for bit in late]
    order += tp_stages + late_stages if tp_first else late_stages + tp_stages
    order += [("ctx", bit) for bit in bits("ctx")[::-1]]
    for axis, bit in order:
        other = swap(held, axis, bit)
        mine = own_bit(axis, bit)
        low = jnp.where(mine == 0, held, other)
        high = jnp.where(mine == 0, other, held)
        if axis == "tp":
            held = jnp.concatenate([low, high], axis=-1)
        else:
            held = jnp.stack([low, high], axis=place)
            place += 1
    return held.reshape(lead, -1, held.shape[-1])


def scatter_sums(grads, tp_first):
    rows_all, cols_all = grads[0].shape
    shards = lax.axis_size("fsdp") * lax.axis_size("ctx")
    rows = rows_all // shards
    held = [g.reshape(lax.axis_size("fsdp"), -1, rows, cols_all) for g in grads]
    first = True
    fs_bits = bits("fsdp")
    tp_stages = [("tp", bit) for bit in bits("tp")[::-1]]
    keep_first = len(fs_bits) // 3
    early = [("fsdp", bit) for bit in fs_bits[:keep_first]]
    late = [("fsdp", bit) for bit in fs_bits[keep_first:][::-1]]
    order = tp_stages + early if tp_first else early + tp_stages
    order += late

    mine = lax.axis_index("ctx")
    pick = lambda which: jnp.stack(
        [lax.dynamic_index_in_dim(g, which, 1, keepdims=False) for g in held]
    )
    recv = swap(pick(1 - mine).astype(BF16), "ctx", 1)
    total = pick(mine) + recv.astype(F32)
    used = {}
    for axis, bit in order:
        mine = own_bit(axis, bit)
        if axis == "tp":
            half = total.shape[-1] // 2
            cut = lambda which: lax.dynamic_slice_in_dim(total, which * half, half, 3)
        else:
            lead, span, rows_here, cols_here = total.shape
            low = 1
            for done in fs_bits:
                if done < bit and done not in used:
                    low *= 2
            view = total.reshape(lead, span // (2 * low), 2, low, rows_here, cols_here)
            cut = lambda which: lax.dynamic_index_in_dim(view, which, 2, keepdims=False).reshape(
                lead, span // 2, rows_here, cols_here
            )
            used[bit] = True
        recv = swap(cut(1 - mine).astype(BF16), axis, bit)
        total = cut(mine) + recv.astype(F32)
    return total[:, 0]


def sum_everywhere(value):
    for axis in ("ctx", "tp", "fsdp"):
        for bit in bits(axis):
            value = value + swap(value, axis, bit)
    return value


def layer_stats(values_in):
    mean_row = jnp.mean(values_in, axis=-1, keepdims=True)
    centered = values_in - mean_row
    inverse = lax.rsqrt(jnp.mean(centered * centered, axis=-1, keepdims=True) + EPSILON)
    return (centered * inverse, inverse)


def layer_back(grad_out, normed, inverse, gain_row):
    scaled = grad_out * gain_row
    return inverse * (
        scaled
        - jnp.mean(scaled, axis=-1, keepdims=True)
        - normed * jnp.mean(scaled * normed, axis=-1, keepdims=True)
    )


def mm(left, right, left_dim, right_dim):
    return lax.dot_general(
        left, right, (((left_dim,), (right_dim,)), ((), ())), preferred_element_type=F32
    )


def head_select():
    row = lax.broadcasted_iota(jnp.int32, (TALL, LANES), 0) // AREA
    lane = lax.broadcasted_iota(jnp.int32, (TALL, LANES), 1) // HEAD_DIM
    return (row == lane).astype(F32)


def spread(value, select):
    return jnp.concatenate([value] * GROUP, axis=0) * select


def fold(tall, select):
    return jnp.sum((tall * select).reshape(GROUP, AREA, LANES), axis=0)


def forward_kernel(
    x_ref, vec_ref, w_ref, bias_ref, mask_ref, tok_ref, q_ref, k_ref, v_ref, p_ref, att_ref, mid_ref, n2_ref
):
    vec = vec_ref[...]
    resid = x_ref[...]
    norm, _ = layer_stats(resid)
    tok = (norm * vec[0:1] + vec[2:3]).astype(BF16)
    tok_ref[...] = tok
    q_ref[...] = (mm(tok, w_ref[0], 1, 0) + vec[6:7]).astype(BF16)
    k_ref[...] = mm(tok, w_ref[1], 1, 0).astype(BF16)
    v_ref[...] = (mm(tok, w_ref[2], 1, 0) + vec[7:8]).astype(BF16)
    select = head_select()
    select_half = select.astype(BF16)

    def window(w, carry):
        here = pl.ds(pl.multiple_of(w * AREA, AREA), AREA)
        mask = mask_ref[w]
        mask_tall = jnp.concatenate([mask] * GROUP, axis=0)
        for g in range(w_ref.shape[2] // LANES):
            part = slice(g * LANES, (g + 1) * LANES)
            tall_q = spread(q_ref[here, part], select_half)
            scores = mm(tall_q, k_ref[here, part], 1, 1) * SCALE
            scores = scores + bias_ref[g * TALL : (g + 1) * TALL, :] + mask_tall
            peak = jnp.max(scores, axis=-1, keepdims=True)
            weight = jnp.exp(scores - peak)
            prob = weight / jnp.sum(weight, axis=-1, keepdims=True)
            p_ref[w, g] = prob
            att_ref[here, part] = fold(
                mm(prob.astype(BF16), v_ref[here, part], 1, 0), select
            ).astype(BF16)
        return carry

    lax.fori_loop(0, PER_STEP, window, 0)
    middle = resid + mm(att_ref[...], w_ref[3], 1, 1) + vec[4:5]
    mid_ref[...] = middle
    norm_two, _ = layer_stats(middle)
    n2_ref[...] = (norm_two * vec[1:2] + vec[3:4]).astype(BF16)


def ffn_kernel(
    mid_ref, n2_ref, cot_ref, up_ref, down_ref, upb_ref, vec_ref,
    out_ref, gm_ref, dup_ref, ddown_ref, dupb_ref, sums_ref, acc_ref, g2_ref
):
    @pl.when(pl.program_id(0) == 0)
    def _():
        dup_ref[...] = jnp.zeros_like(dup_ref)
        ddown_ref[...] = jnp.zeros_like(ddown_ref)
        dupb_ref[...] = jnp.zeros_like(dupb_ref)
        sums_ref[...] = jnp.zeros_like(sums_ref)

    vec = vec_ref[...]
    chunk = 512
    acc_ref[...] = jnp.zeros_like(acc_ref)
    g2_ref[...] = jnp.zeros_like(g2_ref)

    def step(f, carry):
        here = pl.ds(pl.multiple_of(f * chunk, chunk), chunk)
        rows_two = n2_ref[...]
        cot_half = cot_ref[...].astype(BF16)
        pre = mm(rows_two, up_ref[:, here], 1, 0) + upb_ref[:, here]
        phi = 0.5 * (1.0 + lax.erf(pre * (1.0 / math.sqrt(2.0))))
        hidden = (pre * phi).astype(BF16)
        slope = mm(cot_half, down_ref[:, here], 1, 0) * (
            phi + pre * jnp.exp(-0.5 * pre * pre) * (1.0 / math.sqrt(2.0 * math.pi))
        )
        slope_half = slope.astype(BF16)
        acc_ref[...] += mm(hidden, down_ref[:, here], 1, 1)
        g2_ref[...] += mm(slope_half, up_ref[:, here], 1, 1)
        dup_ref[:, here] += mm(rows_two, slope_half, 0, 0)
        ddown_ref[:, here] += mm(cot_half, hidden, 0, 0)
        dupb_ref[:, here] += jnp.sum(slope, axis=0, keepdims=True)
        return carry

    lax.fori_loop(0, up_ref.shape[1] // chunk, step, 0)
    middle = mid_ref[...]
    cot = cot_ref[...]
    out_ref[...] = middle + acc_ref[...] + vec[5:6]
    norm_two, inv_two = layer_stats(middle)
    grad_two = g2_ref[...]
    grad_mid = cot + layer_back(grad_two, norm_two, inv_two, vec[1:2])
    gm_ref[...] = grad_mid
    total = lambda value: jnp.sum(value, axis=0, keepdims=True)
    sums_ref[0:1] += total(grad_two * norm_two)
    sums_ref[1:2] += total(grad_two)
    sums_ref[2:3] += total(grad_mid)
    sums_ref[3:4] += total(cot)


def backward_kernel(
    x_ref, gm_ref, tok_ref, q_ref, k_ref, v_ref, p_ref, att_ref, w_ref, vec_ref,
    img_ref, dw_ref, ds_ref, sums_ref, ga_ref, mixed_ref
):
    @pl.when(pl.program_id(0) == 0)
    def _():
        dw_ref[...] = jnp.zeros_like(dw_ref)
        ds_ref[...] = jnp.zeros_like(ds_ref)
        sums_ref[...] = jnp.zeros_like(sums_ref)

    vec = vec_ref[...]
    grad_mid = gm_ref[...]
    grad_tok = grad_mid.astype(BF16)
    ga_ref[...] = mm(grad_tok, w_ref[3], 1, 0).astype(BF16)
    dw_ref[3] += mm(grad_tok, att_ref[...], 0, 0)
    select = head_select()
    select_half = select.astype(BF16)
    total = lambda value: jnp.sum(value, axis=0, keepdims=True)

    def window(w, carry):
        here = pl.ds(pl.multiple_of(w * AREA, AREA), AREA)
        for g in range(w_ref.shape[2] // LANES):
            part = slice(g * LANES, (g + 1) * LANES)
            tall_q = spread(q_ref[here, part], select_half)
            tall_ga = spread(ga_ref[here, part], select_half)
            prob = p_ref[w, g]
            grad_prob = mm(tall_ga, v_ref[here, part], 1, 1)
            grad_value = mm(prob.astype(BF16), tall_ga, 0, 0)
            weighted = prob * grad_prob
            grad_score = weighted - prob * jnp.sum(weighted, axis=-1, keepdims=True)
            ds_ref[g * TALL : (g + 1) * TALL, :] += grad_score
            score_half = (grad_score * SCALE).astype(BF16)
            grad_query = fold(mm(score_half, k_ref[here, part], 1, 0), select)
            grad_key = mm(score_half, tall_q, 0, 0)
            sums_ref[0:1, part] += total(grad_query)
            sums_ref[1:2, part] += total(grad_value)
            mixed_ref[0, here, part] = grad_query.astype(BF16)
            mixed_ref[1, here, part] = grad_key.astype(BF16)
            mixed_ref[2, here, part] = grad_value.astype(BF16)
        return carry

    lax.fori_loop(0, PER_STEP, window, 0)
    tok = tok_ref[...]
    grad_one = jnp.zeros(grad_mid.shape, F32)
    for j in range(3):
        dw_ref[j] += mm(tok, mixed_ref[j], 0, 0)
        grad_one = grad_one + mm(mixed_ref[j], w_ref[j], 1, 1)
    norm, inv = layer_stats(x_ref[...])
    img_ref[...] = grad_mid + layer_back(grad_one, norm, inv, vec[0:1])
    sums_ref[2:3] += total(grad_one * norm)
    sums_ref[3:4] += total(grad_one)


def to_padded(field):
    images, rows, cols = field.shape[:3]
    rest = field.shape[3:]
    cut = field.reshape(images, rows // WIN, WIN, cols // WIN, WIN, *rest)
    grow = PAD - WIN
    cut = jnp.pad(cut, ((0, 0), (0, 0), (0, grow), (0, 0), (0, grow)) + ((0, 0),) * len(rest))
    order = (0, 1, 3, 2, 4) + tuple(range(5, 5 + len(rest)))
    return cut.transpose(order).reshape(-1, *rest)


def from_padded(tiles, images, rows, cols):
    width = tiles.shape[-1]
    cut = tiles.reshape(images, rows // WIN, cols // WIN, PAD, PAD, width)
    cut = cut.transpose(0, 1, 3, 2, 4, 5)[:, :, :WIN, :, :WIN]
    return cut.reshape(images, rows, cols, width)


def whole_spec(shape):
    return pl.BlockSpec(shape, lambda i: (0,) * len(shape))


def row_spec(cols):
    return pl.BlockSpec((ROWS, cols), lambda i: (i, 0))


PARAMS = dict(compiler_params=pltpu.CompilerParams(vmem_limit_bytes=60 * 1024 * 1024))


def per_device(
    image, cotangent, norm_gain, norm_bias, qkv_weight, qkv_bias, bias_table, bias_index,
    regions, proj_weight, out_bias, up_weight, up_bias, down_weight,
):
    images, band_rows, columns, channels = image.shape
    groups = lax.axis_size("tp")
    table_rows = bias_table.shape[1]
    head_width = qkv_weight.shape[2]
    heads_here = bias_table.shape[0]
    ffn_here = up_bias.shape[0]
    rows_here = qkv_weight.shape[0]

    attn_block = jnp.stack(
        [qkv_weight[:, 0], qkv_weight[:, 1], qkv_weight[:, 2], proj_weight.T]
    )
    ffn_block = jnp.stack([up_weight, down_weight.T])
    vectors = jnp.concatenate([norm_gain, norm_bias, out_bias], axis=0)
    tp_small = jnp.concatenate([qkv_bias.reshape(-1), up_bias, bias_table.reshape(-1)])[None, None]
    small = tp_small
    for bit in bits("tp"):
        other = swap(small, "tp", bit)
        mine = own_bit("tp", bit)
        small = jnp.concatenate(
            [jnp.where(mine == 0, small, other), jnp.where(mine == 0, other, small)], axis=0
        )
    small = small[:, 0]
    held = vectors[None]
    for axis in ("ctx", "fsdp"):
        for bit in bits(axis):
            other = swap(held, axis, bit)
            mine = own_bit(axis, bit)
            held = jnp.concatenate(
                [jnp.where(mine == 0, held, other), jnp.where(mine == 0, other, held)], axis=0
            )
    vec_six = held.transpose(1, 0, 2).reshape(6, channels).astype(F32)
    qb_end = 2 * head_width
    pair_whole = (
        small[:, :qb_end].reshape(groups, 2, head_width).transpose(1, 0, 2).reshape(2, -1).astype(F32)
    )
    upb_whole = small[:, qb_end : qb_end + ffn_here].reshape(1, -1).astype(F32)
    table_whole = small[:, qb_end + ffn_here :].reshape(groups * heads_here, table_rows)
    vec = jnp.concatenate([vec_six, pair_whole], axis=0)

    edge_image, edge_grad = shifted((image[:, :SHIFT], cotangent[:, :SHIFT]), "ctx", -1)
    residual = jnp.concatenate([image[:, SHIFT:], edge_image], axis=1)
    grad_top = jnp.concatenate([cotangent[:, SHIFT:], edge_grad], axis=1)
    edge_image, edge_grad = shifted((residual[:, :, :SHIFT], grad_top[:, :, :SHIFT]), "tp", -1)
    residual = to_padded(jnp.concatenate([residual[:, :, SHIFT:], edge_image], axis=2))
    grad_top = to_padded(jnp.concatenate([grad_top[:, :, SHIFT:], edge_grad], axis=2))
    tokens_all = residual.shape[0]
    windows = tokens_all // AREA

    attn_w = gather_blocks(attn_block, False)
    ffn_w = gather_blocks(ffn_block, True)

    grow = PAD - WIN
    index_pad = jnp.pad(
        bias_index.reshape(WIN, WIN, WIN, WIN), ((0, grow),) * 4, constant_values=-1
    ).reshape(-1)
    one_hot = index_pad[:, None] == jnp.arange(table_rows, dtype=jnp.int32)
    heads_all = table_whole.shape[0]
    rel_bias = jnp.einsum(
        "ht,qt->hq", table_whole, one_hot.astype(BF16), preferred_element_type=F32
    ).reshape(heads_all * AREA, AREA)
    key_spot = jnp.arange(AREA, dtype=jnp.int32)
    key_live = (key_spot // PAD < WIN) & (key_spot % PAD < WIN)
    rel_bias = jnp.where(key_live[None, :], rel_bias, ABSENT)
    col_start = lax.axis_index("tp") * columns
    region_here = lax.dynamic_slice_in_dim(regions, col_start, columns, 1)
    labels = to_padded(region_here[None]).reshape(windows // images, AREA)
    labels = jnp.concatenate([labels] * images, axis=0)
    mask_bias = jnp.where(labels[:, :, None] == labels[:, None, :], 0.0, MASKED).astype(F32)

    steps = tokens_all // ROWS
    sets = heads_all // GROUP
    rows_half = jax.ShapeDtypeStruct((tokens_all, channels), BF16)
    rows_full = jax.ShapeDtypeStruct((tokens_all, channels), F32)
    prob_shape = jax.ShapeDtypeStruct((windows, sets, TALL, AREA), F32)
    prob_spec = pl.BlockSpec((PER_STEP, sets, TALL, AREA), lambda i: (i, 0, 0, 0))
    mask_spec = pl.BlockSpec((PER_STEP, AREA, AREA), lambda i: (i, 0, 0))
    row = row_spec(channels)
    dense = 2 * tokens_all * channels * channels
    tokens, query, key, value, prob, attended, middle, normed_two = pl.pallas_call(
        forward_kernel,
        grid=(steps,),
        in_specs=[
            row, whole_spec(vec.shape), whole_spec(attn_w.shape), whole_spec(rel_bias.shape), mask_spec
        ],
        out_specs=[row, row, row, row, prob_spec, row, row, row],
        out_shape=[rows_half] * 4 + [prob_shape, rows_half, rows_full, rows_half],
        cost_estimate=pl.CostEstimate(
            flops=12 * dense, bytes_accessed=20 * tokens_all * channels, transcendentals=0
        ),
        **PARAMS,
    )(residual, vec, attn_w, rel_bias, mask_bias)

    up_w, down_w = ffn_w[0], ffn_w[1]
    ffn_all = up_w.shape[1]
    output_full, grad_mid, dup, ddown, dupb, sums_two = pl.pallas_call(
        ffn_kernel,
        grid=(steps,),
        in_specs=[
            row, row, row, whole_spec(up_w.shape), whole_spec(down_w.shape),
            whole_spec(upb_whole.shape), whole_spec(vec.shape),
        ],
        out_specs=[
            row, row, whole_spec(up_w.shape), whole_spec(up_w.shape), whole_spec((1, ffn_all)),
            whole_spec((8, channels)),
        ],
        out_shape=[
            rows_full, rows_full, jax.ShapeDtypeStruct(up_w.shape, F32),
            jax.ShapeDtypeStruct(up_w.shape, F32), jax.ShapeDtypeStruct((1, ffn_all), F32),
            jax.ShapeDtypeStruct((8, channels), F32),
        ],
        scratch_shapes=[pltpu.VMEM((ROWS, channels), F32), pltpu.VMEM((ROWS, channels), F32)],
        cost_estimate=pl.CostEstimate(
            flops=24 * dense, bytes_accessed=40 * tokens_all * channels, transcendentals=0
        ),
        **PARAMS,
    )(middle, normed_two, grad_top, up_w, down_w, upb_whole, vec)
    ffn_sums = scatter_sums([dup, ddown], True)

    grad_full, dw, grad_score, sums_one = pl.pallas_call(
        backward_kernel,
        grid=(steps,),
        in_specs=[
            row, row, row, row, row, row, prob_spec, row, whole_spec(attn_w.shape),
            whole_spec(vec.shape),
        ],
        out_specs=[
            row, whole_spec(attn_w.shape), whole_spec(rel_bias.shape), whole_spec((8, channels))
        ],
        out_shape=[
            rows_full, jax.ShapeDtypeStruct(attn_w.shape, F32),
            jax.ShapeDtypeStruct(rel_bias.shape, F32), jax.ShapeDtypeStruct((8, channels), F32),
        ],
        scratch_shapes=[
            pltpu.VMEM((ROWS, channels), BF16), pltpu.VMEM((3, ROWS, channels), BF16)
        ],
        cost_estimate=pl.CostEstimate(
            flops=24 * dense, bytes_accessed=40 * tokens_all * channels, transcendentals=0
        ),
        **PARAMS,
    )(residual, grad_mid, tokens, query, key, value, prob, attended, attn_w, vec)
    attn_sums = scatter_sums([dw[0], dw[1], dw[2], dw[3]], False)

    table_all = jnp.einsum(
        "hq,qt->ht",
        grad_score.reshape(heads_all, AREA * AREA),
        one_hot.astype(F32),
        precision=lax.Precision.HIGHEST,
    )
    small_total = sum_everywhere(
        jnp.concatenate(
            [
                sums_one[:4].reshape(-1), sums_two[:4].reshape(-1), dupb.reshape(-1),
                table_all.reshape(-1),
            ]
        )
    )
    cut = 4 * channels
    one_sum = small_total[:cut].reshape(4, channels)
    two_sum = small_total[cut : 2 * cut].reshape(4, channels)
    upb_sum = small_total[2 * cut : 2 * cut + ffn_all]
    table_sum = small_total[2 * cut + ffn_all :].reshape(heads_all, table_rows)
    tp_index = lax.axis_index("tp")
    shard = lax.axis_index("fsdp") * lax.axis_size("ctx") + lax.axis_index("ctx")
    take = lambda value: lax.dynamic_slice_in_dim(value, shard * rows_here, rows_here, 1)
    gain_grad = take(jnp.stack([one_sum[2], two_sum[0]]))
    bias_grad = take(jnp.stack([one_sum[3], two_sum[1]]))
    out_grad = take(jnp.stack([two_sum[2], two_sum[3]]))
    qkv_bias_grad = lax.dynamic_slice_in_dim(one_sum[:2], tp_index * head_width, head_width, 1)
    up_bias_grad = lax.dynamic_slice_in_dim(upb_sum, tp_index * ffn_here, ffn_here, 0)
    table_grad = lax.dynamic_slice_in_dim(table_sum, tp_index * heads_here, heads_here, 0)

    output_full = from_padded(output_full, images, band_rows, columns)
    grad_full = from_padded(grad_full, images, band_rows, columns)
    edge_out, edge_back = shifted((output_full[:, :, -SHIFT:], grad_full[:, :, -SHIFT:]), "tp", 1)
    output_shift = jnp.concatenate([edge_out, output_full[:, :, :-SHIFT]], axis=2)
    grad_start = jnp.concatenate([edge_back, grad_full[:, :, :-SHIFT]], axis=2)
    edge_out, edge_back = shifted((output_shift[:, -SHIFT:], grad_start[:, -SHIFT:]), "ctx", 1)
    output = jnp.concatenate([edge_out, output_shift[:, :-SHIFT]], axis=1)
    image_grad = jnp.concatenate([edge_back, grad_start[:, :-SHIFT]], axis=1)
    return (
        output, image_grad, gain_grad, bias_grad,
        jnp.stack([attn_sums[0], attn_sums[1], attn_sums[2]], axis=1),
        qkv_bias_grad, table_grad, attn_sums[3].T, out_grad, ffn_sums[0], up_bias_grad,
        ffn_sums[1].T,
    )


def solution(mesh):
    in_specs = (
        P("fsdp", "ctx", "tp", None),
        P("fsdp", "ctx", "tp", None),
        P(None, ("fsdp", "ctx")),
        P(None, ("fsdp", "ctx")),
        P(("fsdp", "ctx"), None, "tp"),
        P(None, "tp"),
        P("tp", None),
        P(),
        P("ctx", None),
        P("tp", ("fsdp", "ctx")),
        P(None, ("fsdp", "ctx")),
        P(("fsdp", "ctx"), "tp"),
        P("tp"),
        P("tp", ("fsdp", "ctx")),
    )
    out_specs = (
        P("fsdp", "ctx", "tp", None),
        P("fsdp", "ctx", "tp", None),
        P(None, ("fsdp", "ctx")),
        P(None, ("fsdp", "ctx")),
        P(("fsdp", "ctx"), None, "tp"),
        P(None, "tp"),
        P("tp", None),
        P("tp", ("fsdp", "ctx")),
        P(None, ("fsdp", "ctx")),
        P(("fsdp", "ctx"), "tp"),
        P("tp"),
        P("tp", ("fsdp", "ctx")),
    )
    return jax.shard_map(
        per_device, mesh=mesh, in_specs=in_specs, out_specs=out_specs, check_vma=False
    )
```

```python
import math

import jax
import jax.numpy as jnp
from jax import lax
from jax.experimental import pallas as pl
from jax.experimental.pallas import tpu as pltpu
from jax.sharding import PartitionSpec as P

HEAD_DIM = 32
WIN = 7
PAD = 8
AREA = PAD * PAD
SHIFT = 3
GROUP = 8
LANES = GROUP * HEAD_DIM
TALL = GROUP * AREA
PER_STEP = 4
ROWS = PER_STEP * AREA

EPSILON = 1e-05
MASKED = -100.0
ABSENT = -1e30
SCALE = 1.0 / math.sqrt(HEAD_DIM)
F32 = jnp.float32
BF16 = jnp.bfloat16


def shifted(value, axis, steps):
    count = lax.axis_size(axis)
    pairs = [(source, (source + steps) % count) for source in range(count)]
    return lax.ppermute(value, axis, pairs)


def bits(axis):
    return [1 << k for k in range(lax.axis_size(axis).bit_length() - 1)]


def swap(value, axis, bit):
    return lax.ppermute(value, axis, [(i, i ^ bit) for i in range(lax.axis_size(axis))])


def own_bit(axis, bit):
    return (lax.axis_index(axis) // bit) % 2


def split_bits():
    high_first = bits("fsdp")[::-1]
    cut = len(high_first) - len(high_first) // 3
    return [("fsdp", bit) for bit in high_first[:cut]], [("fsdp", bit) for bit in high_first[cut:]]


def gather_steps(held, order):
    for axis, bit in order:
        other = swap(held, axis, bit)
        mine = own_bit(axis, bit)
        low = jnp.where(mine == 0, held, other)
        high = jnp.where(mine == 0, other, held)
        if axis == "tp":
            held = jnp.concatenate([low, high], axis=-1)
        else:
            held = jnp.stack([low, high], axis=held.ndim - 2)
    return held


def first_halves(grads):
    lead, rows_all, cols_all = grads[0].shape
    span = lax.axis_size("fsdp")
    pair = lax.axis_size("ctx")
    rows = rows_all // (span * pair)
    mine = lax.axis_index("ctx")
    cut = lambda g, which: lax.dynamic_index_in_dim(
        g.reshape(lead, span, pair, rows, cols_all), which, 2, keepdims=False
    )
    pick = lambda which: sum(cut(g, which) for g in grads)
    return pick(1 - mine).astype(BF16), pick(mine)


def joined(send, keep, axis, bit):
    return keep + swap(send, axis, bit).astype(F32)


def halves(total, axis, bit, used):
    mine = own_bit(axis, bit)
    if axis == "tp":
        half = total.shape[-1] // 2
        cut = lambda which: lax.dynamic_slice_in_dim(total, which * half, half, 3)
    else:
        lead, span, rows_here, cols_here = total.shape
        low = 1
        for other_bit in bits("fsdp"):
            if other_bit < bit and other_bit not in used:
                low *= 2
        view = total.reshape(lead, span // (2 * low), 2, low, rows_here, cols_here)
        cut = lambda which: lax.dynamic_index_in_dim(view, which, 2, keepdims=False).reshape(
            lead, span // 2, rows_here, cols_here
        )
    return cut(1 - mine).astype(BF16), cut(mine)


def scatter_steps(total, order, used):
    used = set(used)
    for axis, bit in order:
        total = joined(*halves(total, axis, bit, used), axis, bit)
        if axis == "fsdp":
            used.add(bit)
    return total


def layer_stats(values_in):
    mean_row = jnp.mean(values_in, axis=-1, keepdims=True)
    centered = values_in - mean_row
    inverse = lax.rsqrt(jnp.mean(centered * centered, axis=-1, keepdims=True) + EPSILON)
    return (centered * inverse, inverse)


def layer_back(grad_out, normed, inverse, gain_row):
    scaled = grad_out * gain_row
    return inverse * (
        scaled
        - jnp.mean(scaled, axis=-1, keepdims=True)
        - normed * jnp.mean(scaled * normed, axis=-1, keepdims=True)
    )


def mm(left, right, left_dim, right_dim):
    return lax.dot_general(
        left, right, (((left_dim,), (right_dim,)), ((), ())), preferred_element_type=F32
    )


def head_select():
    row = lax.broadcasted_iota(jnp.int32, (TALL, LANES), 0) // AREA
    lane = lax.broadcasted_iota(jnp.int32, (TALL, LANES), 1) // HEAD_DIM
    return (row == lane).astype(F32)


def spread(value, select):
    return jnp.concatenate([value] * GROUP, axis=0) * select


def fold(tall, select):
    return jnp.sum((tall * select).reshape(GROUP, AREA, LANES), axis=0)


def forward_kernel(
    x_ref, vec_ref, w_ref, bias_ref, mask_ref, *rest
):
    tok_ref, q_ref, k_ref, v_ref, p_ref, att_ref, mid_ref, n2_ref = rest[-8:]
    vec = vec_ref[...]
    resid = x_ref[...]
    norm, _ = layer_stats(resid)
    tok = (norm * vec[0:1] + vec[2:3]).astype(BF16)
    tok_ref[...] = tok
    q_ref[...] = (mm(tok, w_ref[0], 1, 0) + vec[6:7]).astype(BF16)
    k_ref[...] = mm(tok, w_ref[1], 1, 0).astype(BF16)
    v_ref[...] = (mm(tok, w_ref[2], 1, 0) + vec[7:8]).astype(BF16)
    select = head_select()
    select_half = select.astype(BF16)

    def window(w, carry):
        here = pl.ds(pl.multiple_of(w * AREA, AREA), AREA)
        mask = mask_ref[w]
        mask_tall = jnp.concatenate([mask] * GROUP, axis=0)
        for g in range(w_ref.shape[2] // LANES):
            part = slice(g * LANES, (g + 1) * LANES)
            tall_q = spread(q_ref[here, part], select_half)
            scores = mm(tall_q, k_ref[here, part], 1, 1) * SCALE
            scores = scores + bias_ref[g * TALL : (g + 1) * TALL, :] + mask_tall
            peak = jnp.max(scores, axis=-1, keepdims=True)
            weight = jnp.exp(scores - peak)
            prob = weight / jnp.sum(weight, axis=-1, keepdims=True)
            p_ref[w, g] = prob
            att_ref[here, part] = fold(
                mm(prob.astype(BF16), v_ref[here, part], 1, 0), select
            ).astype(BF16)
        return carry

    lax.fori_loop(0, PER_STEP, window, 0, unroll=True)
    middle = resid + mm(att_ref[...], w_ref[3], 1, 1) + vec[4:5]
    mid_ref[...] = middle
    norm_two, _ = layer_stats(middle)
    n2_ref[...] = (norm_two * vec[1:2] + vec[3:4]).astype(BF16)


def ffn_kernel(
    mid_ref, n2_ref, cot_ref, up_ref, down_ref, upb_ref, vec_ref,
    out_ref, gm_ref, dffn_ref, dupb_ref, sums_ref, acc_ref, g2_ref
):
    @pl.when(pl.program_id(0) == 0)
    def _():
        dffn_ref[...] = jnp.zeros_like(dffn_ref)
        dupb_ref[...] = jnp.zeros_like(dupb_ref)
        sums_ref[...] = jnp.zeros_like(sums_ref)

    vec = vec_ref[...]
    chunk = 512
    acc_ref[...] = jnp.zeros_like(acc_ref)
    g2_ref[...] = jnp.zeros_like(g2_ref)

    def step(f, carry):
        here = pl.ds(pl.multiple_of(f * chunk, chunk), chunk)
        rows_two = n2_ref[...]
        cot_half = cot_ref[...].astype(BF16)
        pre = mm(rows_two, up_ref[:, here], 1, 0) + upb_ref[:, here]
        phi = 0.5 * (1.0 + lax.erf(pre * (1.0 / math.sqrt(2.0))))
        hidden = (pre * phi).astype(BF16)
        slope = mm(cot_half, down_ref[:, here], 1, 0) * (
            phi + pre * jnp.exp(-0.5 * pre * pre) * (1.0 / math.sqrt(2.0 * math.pi))
        )
        slope_half = slope.astype(BF16)
        acc_ref[...] += mm(hidden, down_ref[:, here], 1, 1)
        g2_ref[...] += mm(slope_half, up_ref[:, here], 1, 1)
        dffn_ref[0, :, here] += mm(rows_two, slope_half, 0, 0)
        dffn_ref[1, :, here] += mm(cot_half, hidden, 0, 0)
        dupb_ref[:, here] += jnp.sum(slope, axis=0, keepdims=True)
        return carry

    lax.fori_loop(0, up_ref.shape[1] // chunk, step, 0)
    middle = mid_ref[...]
    cot = cot_ref[...]
    out_ref[...] = middle + acc_ref[...] + vec[5:6]
    norm_two, inv_two = layer_stats(middle)
    grad_two = g2_ref[...]
    grad_mid = cot + layer_back(grad_two, norm_two, inv_two, vec[1:2])
    gm_ref[...] = grad_mid
    total = lambda value: jnp.sum(value, axis=0, keepdims=True)
    sums_ref[0:1] += total(grad_two * norm_two)
    sums_ref[1:2] += total(grad_two)
    sums_ref[2:3] += total(grad_mid)
    sums_ref[3:4] += total(cot)


def backward_kernel(
    x_ref, gm_ref, tok_ref, q_ref, k_ref, v_ref, p_ref, att_ref, w_ref, vec_ref, *rest
):
    img_ref, dw_ref, ds_ref, sums_ref, ga_ref, mixed_ref = rest[-6:]

    @pl.when(pl.program_id(0) == 0)
    def _():
        dw_ref[...] = jnp.zeros_like(dw_ref)
        ds_ref[...] = jnp.zeros_like(ds_ref)
        sums_ref[...] = jnp.zeros_like(sums_ref)

    vec = vec_ref[...]
    grad_mid = gm_ref[...]
    grad_tok = grad_mid.astype(BF16)
    ga_ref[...] = mm(grad_tok, w_ref[3], 1, 0).astype(BF16)
    dw_ref[3] += mm(grad_tok, att_ref[...], 0, 0)
    select = head_select()
    select_half = select.astype(BF16)
    total = lambda value: jnp.sum(value, axis=0, keepdims=True)

    def window(w, carry):
        here = pl.ds(pl.multiple_of(w * AREA, AREA), AREA)
        for g in range(w_ref.shape[2] // LANES):
            part = slice(g * LANES, (g + 1) * LANES)
            tall_q = spread(q_ref[here, part], select_half)
            tall_ga = spread(ga_ref[here, part], select_half)
            prob = p_ref[w, g]
            grad_prob = mm(tall_ga, v_ref[here, part], 1, 1)
            grad_value = mm(prob.astype(BF16), tall_ga, 0, 0)
            weighted = prob * grad_prob
            grad_score = weighted - prob * jnp.sum(weighted, axis=-1, keepdims=True)
            ds_ref[g * TALL : (g + 1) * TALL, :] += grad_score
            score_half = (grad_score * SCALE).astype(BF16)
            grad_query = fold(mm(score_half, k_ref[here, part], 1, 0), select)
            grad_key = mm(score_half, tall_q, 0, 0)
            sums_ref[0:1, part] += total(grad_query)
            sums_ref[1:2, part] += total(grad_value)
            mixed_ref[0, here, part] = grad_query.astype(BF16)
            mixed_ref[1, here, part] = grad_key.astype(BF16)
            mixed_ref[2, here, part] = grad_value.astype(BF16)
        return carry

    lax.fori_loop(0, PER_STEP, window, 0, unroll=True)
    tok = tok_ref[...]
    grad_one = jnp.zeros(grad_mid.shape, F32)
    for j in range(3):
        dw_ref[j] += mm(tok, mixed_ref[j], 0, 0)
        grad_one = grad_one + mm(mixed_ref[j], w_ref[j], 1, 1)
    norm, inv = layer_stats(x_ref[...])
    img_ref[...] = grad_mid + layer_back(grad_one, norm, inv, vec[0:1])
    sums_ref[2:3] += total(grad_one * norm)
    sums_ref[3:4] += total(grad_one)


def to_padded(field):
    images, rows, cols = field.shape[:3]
    rest = field.shape[3:]
    cut = field.reshape(images, rows // WIN, WIN, cols // WIN, WIN, *rest)
    grow = PAD - WIN
    cut = jnp.pad(cut, ((0, 0), (0, 0), (0, grow), (0, 0), (0, grow)) + ((0, 0),) * len(rest))
    order = (0, 1, 3, 2, 4) + tuple(range(5, 5 + len(rest)))
    return cut.transpose(order).reshape(-1, *rest)


def from_padded(tiles, images, rows, cols):
    width = tiles.shape[-1]
    cut = tiles.reshape(images, rows // WIN, cols // WIN, PAD, PAD, width)
    cut = cut.transpose(0, 1, 3, 2, 4, 5)[:, :, :WIN, :, :WIN]
    return cut.reshape(images, rows, cols, width)


def whole_spec(shape):
    return pl.BlockSpec(shape, lambda i: (0,) * len(shape))


def row_spec(cols, first=0):
    return pl.BlockSpec((ROWS, cols), lambda i: (i + first, 0))


PARAMS = dict(compiler_params=pltpu.CompilerParams(vmem_limit_bytes=60 * 1024 * 1024))


def per_device(
    image, cotangent, norm_gain, norm_bias, qkv_weight, qkv_bias, bias_table, bias_index,
    regions, proj_weight, out_bias, up_weight, up_bias, down_weight,
):
    images, band_rows, columns, channels = image.shape
    groups = lax.axis_size("tp")
    table_rows = bias_table.shape[1]
    head_width = qkv_weight.shape[2]
    heads_here = bias_table.shape[0]
    ffn_here = up_bias.shape[0]
    rows_here = qkv_weight.shape[0]

    shards = lax.axis_size("fsdp") * lax.axis_size("ctx")
    small_parts = [
        norm_gain.reshape(-1), norm_bias.reshape(-1), out_bias.reshape(-1), qkv_bias.reshape(-1),
        up_bias, bias_table.reshape(-1),
    ]
    small_len = sum(part.shape[0] for part in small_parts)
    small_rows = -(-small_len // (16 * head_width)) * 16
    small_parts.append(jnp.zeros((small_rows * head_width - small_len,), BF16))
    attn_block = jnp.concatenate(
        [
            qkv_weight[:, 0], qkv_weight[:, 1], qkv_weight[:, 2], proj_weight.T,
            jnp.concatenate(small_parts).reshape(small_rows, head_width),
        ],
        axis=0,
    )
    ffn_block = jnp.stack([up_weight, down_weight.T])
    far, near = split_bits()
    across = [("tp", bit) for bit in bits("tp")]
    last = [("ctx", bit) for bit in bits("ctx")[::-1]]
    attn_all = gather_steps(attn_block, far + near + across + last)
    attn_all = attn_all.reshape(shards, 4 * rows_here + small_rows, groups * head_width)
    attn_w = (
        attn_all[:, : 4 * rows_here]
        .reshape(shards, 4, rows_here, channels)
        .transpose(1, 0, 2, 3)
        .reshape(4, channels, channels)
    )
    ffn_far = gather_steps(ffn_block, far)
    up_held = gather_steps(ffn_far[0], across)
    down_held = gather_steps(ffn_far[1], near)
    up_held, down_held, attn_w = lax.optimization_barrier((up_held, down_held, attn_w))
    up_held = gather_steps(up_held, near)
    down_held = gather_steps(down_held, across)

    small = (
        attn_all[:, 4 * rows_here :]
        .reshape(shards, small_rows, groups, head_width)
        .transpose(0, 2, 1, 3)
        .reshape(shards, groups, -1)
    )
    v_end = 6 * rows_here
    vec_six = (
        small[:, 0, :v_end].reshape(shards, 6, rows_here).transpose(1, 0, 2).reshape(6, channels)
    ).astype(F32)
    small = small[0, :, v_end:small_len]
    qb_end = 2 * head_width
    pair_whole = (
        small[:, :qb_end].reshape(groups, 2, head_width).transpose(1, 0, 2).reshape(2, -1).astype(F32)
    )
    upb_whole = small[:, qb_end : qb_end + ffn_here].reshape(1, -1).astype(F32)
    table_whole = small[:, qb_end + ffn_here :].reshape(groups * heads_here, table_rows)
    vec = jnp.concatenate([vec_six, pair_whole], axis=0)

    edge_image, edge_grad = shifted((image[:, :SHIFT], cotangent[:, :SHIFT]), "ctx", -1)
    residual = jnp.concatenate([image[:, SHIFT:], edge_image], axis=1)
    grad_top = jnp.concatenate([cotangent[:, SHIFT:], edge_grad], axis=1)
    edge_image, edge_grad = shifted((residual[:, :, :SHIFT], grad_top[:, :, :SHIFT]), "tp", -1)
    residual = to_padded(jnp.concatenate([residual[:, :, SHIFT:], edge_image], axis=2))
    grad_top = to_padded(jnp.concatenate([grad_top[:, :, SHIFT:], edge_grad], axis=2))
    tokens_all = residual.shape[0]
    windows = tokens_all // AREA

    grow = PAD - WIN
    index_pad = jnp.pad(
        bias_index.reshape(WIN, WIN, WIN, WIN), ((0, grow),) * 4, constant_values=-1
    ).reshape(-1)
    one_hot = index_pad[:, None] == jnp.arange(table_rows, dtype=jnp.int32)
    heads_all = table_whole.shape[0]
    rel_bias = jnp.einsum(
        "ht,qt->hq", table_whole, one_hot.astype(BF16), preferred_element_type=F32
    ).reshape(heads_all * AREA, AREA)
    key_spot = jnp.arange(AREA, dtype=jnp.int32)
    key_live = (key_spot // PAD < WIN) & (key_spot % PAD < WIN)
    rel_bias = jnp.where(key_live[None, :], rel_bias, ABSENT)
    col_start = lax.axis_index("tp") * columns
    region_here = lax.dynamic_slice_in_dim(regions, col_start, columns, 1)
    labels = to_padded(region_here[None]).reshape(windows // images, AREA)
    labels = jnp.concatenate([labels] * images, axis=0)
    mask_bias = jnp.where(labels[:, :, None] == labels[:, None, :], 0.0, MASKED).astype(F32)

    steps = tokens_all // ROWS
    sets = heads_all // GROUP
    half_steps = [steps] if steps < 2 else [steps // 2, steps - steps // 2]
    rows_full = jax.ShapeDtypeStruct((tokens_all, channels), F32)
    rows_all_half = jax.ShapeDtypeStruct((tokens_all, channels), BF16)
    prob_spec = pl.BlockSpec((PER_STEP, sets, TALL, AREA), lambda i: (i, 0, 0, 0))
    row = row_spec(channels)
    anywhere = pl.BlockSpec(memory_space=pl.ANY)
    dense = 2 * ROWS * channels * channels
    moved = ROWS * channels

    saved = []
    carried = ()
    for part, count in enumerate(half_steps):
        first = part * half_steps[0]
        placed = row_spec(channels, first)
        rows_half = jax.ShapeDtypeStruct((count * ROWS, channels), BF16)
        prob_shape = jax.ShapeDtypeStruct((count * PER_STEP, sets, TALL, AREA), F32)
        mask_spec = pl.BlockSpec((PER_STEP, AREA, AREA), lambda i, first=first: (i + first, 0, 0))
        mask_here = mask_bias
        if part:
            up_held, down_held, mask_here = lax.optimization_barrier((up_held, down_held, mask_bias))
        *kept, middle, normed_two = pl.pallas_call(
            forward_kernel,
            grid=(count,),
            in_specs=[
                placed, whole_spec(vec.shape), whole_spec(attn_w.shape), whole_spec(rel_bias.shape),
                mask_spec,
            ]
            + [anywhere] * len(carried),
            out_specs=[row, row, row, row, prob_spec, row, placed, placed],
            out_shape=[rows_half] * 4 + [prob_shape, rows_half, rows_full, rows_all_half],
            input_output_aliases={5 + n: 6 + n for n in range(len(carried))},
            cost_estimate=pl.CostEstimate(
                flops=40 * count * dense, bytes_accessed=20 * count * moved, transcendentals=0
            ),
            **PARAMS,
        )(residual, vec, attn_w, rel_bias, mask_here, *carried)
        carried = (middle, normed_two)
        saved.append(kept)

    up_w = gather_steps(up_held, last).reshape(channels, -1)
    down_w = gather_steps(down_held, last).reshape(channels, -1)
    ffn_all = up_w.shape[1]
    output_full, grad_mid, dffn, dupb, sums_two = pl.pallas_call(
        ffn_kernel,
        grid=(steps,),
        in_specs=[
            row, row, row, whole_spec(up_w.shape), whole_spec(down_w.shape),
            whole_spec(upb_whole.shape), whole_spec(vec.shape),
        ],
        out_specs=[
            row, row, whole_spec((2,) + up_w.shape), whole_spec((1, ffn_all)),
            whole_spec((8, channels)),
        ],
        out_shape=[
            rows_full, rows_full, jax.ShapeDtypeStruct((2,) + up_w.shape, F32), jax.ShapeDtypeStruct((1, ffn_all), F32),
            jax.ShapeDtypeStruct((8, channels), F32),
        ],
        scratch_shapes=[pltpu.VMEM((ROWS, channels), F32), pltpu.VMEM((ROWS, channels), F32)],
        cost_estimate=pl.CostEstimate(
            flops=60 * steps * dense, bytes_accessed=40 * steps * moved, transcendentals=0
        ),
        **PARAMS,
    )(middle, normed_two, grad_top, up_w, down_w, upb_whole, vec)
    across_high = across[::-1]
    ffn_total = joined(*first_halves([dffn]), "ctx", 1)
    orders = (across_high + near, near + across_high)

    weight_parts, score_parts, sum_parts = [], [], []
    carried = ()
    for part, count in enumerate(half_steps):
        first = part * half_steps[0]
        placed = row_spec(channels, first)
        gm_here = grad_mid
        if part:
            up_cut = halves(ffn_total[:1], *orders[0][0], ())
            down_cut = halves(ffn_total[1:], *orders[1][0], ())
            up_cut, down_cut, gm_here = lax.optimization_barrier((up_cut, down_cut, grad_mid))
            up_total = joined(*up_cut, *orders[0][0])
            down_total = joined(*down_cut, *orders[1][0])
            orders = (orders[0][1:], orders[1][1:])
        grad_full, dw, grad_score, sums_one = pl.pallas_call(
            backward_kernel,
            grid=(count,),
            in_specs=[
                placed, placed, row, row, row, row, prob_spec, row, whole_spec(attn_w.shape),
                whole_spec(vec.shape),
            ]
            + [anywhere] * len(carried),
            out_specs=[
                placed, whole_spec(attn_w.shape), whole_spec(rel_bias.shape),
                whole_spec((8, channels)),
            ],
            out_shape=[
                rows_full, jax.ShapeDtypeStruct(attn_w.shape, F32),
                jax.ShapeDtypeStruct(rel_bias.shape, F32),
                jax.ShapeDtypeStruct((8, channels), F32),
            ],
            input_output_aliases={10 + n: n for n in range(len(carried))},
            scratch_shapes=[
                pltpu.VMEM((ROWS, channels), BF16), pltpu.VMEM((3, ROWS, channels), BF16)
            ],
            cost_estimate=pl.CostEstimate(
                flops=60 * count * dense, bytes_accessed=40 * count * moved, transcendentals=0
            ),
            **PARAMS,
        )(residual, gm_here, *saved[part], attn_w, vec, *carried)
        carried = (grad_full,)
        weight_parts.append(dw)
        score_parts.append(grad_score)
        sum_parts.append(sums_one)
    if len(half_steps) == 1:
        up_total, down_total = ffn_total[:1], ffn_total[1:]
    else:
        up_total, down_total, weight_parts, score_parts, sum_parts, grad_full = (
            lax.optimization_barrier(
                (up_total, down_total, weight_parts, score_parts, sum_parts, grad_full)
            )
        )
    sums_one = sum(sum_parts)
    table_all = jnp.einsum(
        "hq,qt->ht",
        sum(score_parts).reshape(heads_all, AREA * AREA),
        one_hot.astype(F32),
        precision=lax.Precision.HIGHEST,
    )
    small_total = jnp.concatenate(
        [
            sums_one[:4].reshape(-1), sums_two[:4].reshape(-1), dupb.reshape(-1),
            table_all.reshape(-1),
        ]
    )
    small_plan = [(axis, bit) for axis in ("ctx", "tp", "fsdp") for bit in bits(axis)]
    attn_plan = [("ctx", 1)] + near + across_high + far
    up_plan, down_plan, ffn_plan = list(orders[0]), list(orders[1]), list(far)
    up_used = {bit for axis, bit in near if (axis, bit) not in up_plan}
    down_used = {bit for axis, bit in near if (axis, bit) not in down_plan}
    ffn_used = {bit for _, bit in near}
    attn_used = set()
    attn_sums, ffn_sums = None, None
    while attn_plan or small_plan or up_plan or down_plan or ffn_plan:
        if attn_plan:
            move = attn_plan.pop(0)
            if attn_sums is None:
                attn_sums = joined(*first_halves(weight_parts), *move)
            else:
                attn_sums = scatter_steps(attn_sums, [move], attn_used)
                attn_used |= {move[1]} if move[0] == "fsdp" else set()
        if small_plan:
            axis, bit = small_plan.pop(0)
            small_total = small_total + swap(small_total, axis, bit)
        if up_plan or down_plan:
            if up_plan:
                move = up_plan.pop(0)
                up_total = scatter_steps(up_total, [move], up_used)
                up_used |= {move[1]} if move[0] == "fsdp" else set()
            if down_plan:
                move = down_plan.pop(0)
                down_total = scatter_steps(down_total, [move], down_used)
                down_used |= {move[1]} if move[0] == "fsdp" else set()
            up_total, down_total, attn_sums, small_total = lax.optimization_barrier(
                (up_total, down_total, attn_sums, small_total)
            )
        else:
            if ffn_sums is None:
                ffn_sums = jnp.concatenate([up_total, down_total], axis=0)
            if ffn_plan:
                move = ffn_plan.pop(0)
                ffn_sums = scatter_steps(ffn_sums, [move], ffn_used)
                ffn_used.add(move[1])
            ffn_sums, attn_sums, small_total = lax.optimization_barrier(
                (ffn_sums, attn_sums, small_total)
            )
    if ffn_sums is None:
        ffn_sums = jnp.concatenate([up_total, down_total], axis=0)
    ffn_sums, attn_sums = ffn_sums[:, 0], attn_sums[:, 0]
    cut = 4 * channels
    one_sum = small_total[:cut].reshape(4, channels)
    two_sum = small_total[cut : 2 * cut].reshape(4, channels)
    upb_sum = small_total[2 * cut : 2 * cut + ffn_all]
    table_sum = small_total[2 * cut + ffn_all :].reshape(heads_all, table_rows)
    tp_index = lax.axis_index("tp")
    shard = lax.axis_index("fsdp") * lax.axis_size("ctx") + lax.axis_index("ctx")
    take = lambda value: lax.dynamic_slice_in_dim(value, shard * rows_here, rows_here, 1)
    gain_grad = take(jnp.stack([one_sum[2], two_sum[0]]))
    bias_grad = take(jnp.stack([one_sum[3], two_sum[1]]))
    out_grad = take(jnp.stack([two_sum[2], two_sum[3]]))
    qkv_bias_grad = lax.dynamic_slice_in_dim(one_sum[:2], tp_index * head_width, head_width, 1)
    up_bias_grad = lax.dynamic_slice_in_dim(upb_sum, tp_index * ffn_here, ffn_here, 0)
    table_grad = lax.dynamic_slice_in_dim(table_sum, tp_index * heads_here, heads_here, 0)

    output_full = from_padded(output_full, images, band_rows, columns)
    grad_full = from_padded(grad_full, images, band_rows, columns)
    edge_out, edge_back = shifted((output_full[:, :, -SHIFT:], grad_full[:, :, -SHIFT:]), "tp", 1)
    output_shift = jnp.concatenate([edge_out, output_full[:, :, :-SHIFT]], axis=2)
    grad_start = jnp.concatenate([edge_back, grad_full[:, :, :-SHIFT]], axis=2)
    edge_out, edge_back = shifted((output_shift[:, -SHIFT:], grad_start[:, -SHIFT:]), "ctx", 1)
    output = jnp.concatenate([edge_out, output_shift[:, :-SHIFT]], axis=1)
    image_grad = jnp.concatenate([edge_back, grad_start[:, :-SHIFT]], axis=1)
    return (
        output, image_grad, gain_grad, bias_grad,
        jnp.stack([attn_sums[0], attn_sums[1], attn_sums[2]], axis=1),
        qkv_bias_grad, table_grad, attn_sums[3].T, out_grad, ffn_sums[0], up_bias_grad,
        ffn_sums[1].T,
    )


def solution(mesh):
    in_specs = (
        P("fsdp", "ctx", "tp", None),
        P("fsdp", "ctx", "tp", None),
        P(None, ("fsdp", "ctx")),
        P(None, ("fsdp", "ctx")),
        P(("fsdp", "ctx"), None, "tp"),
        P(None, "tp"),
        P("tp", None),
        P(),
        P("ctx", None),
        P("tp", ("fsdp", "ctx")),
        P(None, ("fsdp", "ctx")),
        P(("fsdp", "ctx"), "tp"),
        P("tp"),
        P("tp", ("fsdp", "ctx")),
    )
    out_specs = (
        P("fsdp", "ctx", "tp", None),
        P("fsdp", "ctx", "tp", None),
        P(None, ("fsdp", "ctx")),
        P(None, ("fsdp", "ctx")),
        P(("fsdp", "ctx"), None, "tp"),
        P(None, "tp"),
        P("tp", None),
        P("tp", ("fsdp", "ctx")),
        P(None, ("fsdp", "ctx")),
        P(("fsdp", "ctx"), "tp"),
        P("tp"),
        P("tp", ("fsdp", "ctx")),
    )
    return jax.shard_map(
        per_device, mesh=mesh, in_specs=in_specs, out_specs=out_specs, check_vma=False
    )
```

```python
import math

import jax
import jax.numpy as jnp
from jax import lax
from jax.experimental import pallas as pl
from jax.experimental.pallas import tpu as pltpu
from jax.sharding import PartitionSpec as P

HEAD_DIM = 32
WIN = 7
PAD = 8
AREA = PAD * PAD
SHIFT = 3
GROUP = 8
LANES = GROUP * HEAD_DIM
TALL = GROUP * AREA
PER_STEP = 4
ROWS = PER_STEP * AREA

EPSILON = 1e-05
MASKED = -100.0
ABSENT = -1e30
SCALE = 1.0 / math.sqrt(HEAD_DIM)
F32 = jnp.float32
BF16 = jnp.bfloat16


def shifted(value, axis, steps):
    count = lax.axis_size(axis)
    pairs = [(source, (source + steps) % count) for source in range(count)]
    return lax.ppermute(value, axis, pairs)


def bits(axis):
    return [1 << k for k in range(lax.axis_size(axis).bit_length() - 1)]


def swap(value, axis, bit):
    return lax.ppermute(value, axis, [(i, i ^ bit) for i in range(lax.axis_size(axis))])


def own_bit(axis, bit):
    return (lax.axis_index(axis) // bit) % 2


def split_bits():
    high_first = bits("fsdp")[::-1]
    cut = len(high_first) - len(high_first) // 3
    return [("fsdp", bit) for bit in high_first[:cut]], [("fsdp", bit) for bit in high_first[cut:]]


def gather_steps(held, order):
    for axis, bit in order:
        other = swap(held, axis, bit)
        mine = own_bit(axis, bit)
        low = jnp.where(mine == 0, held, other)
        high = jnp.where(mine == 0, other, held)
        if axis == "tp":
            held = jnp.concatenate([low, high], axis=-1)
        else:
            held = jnp.stack([low, high], axis=held.ndim - 2)
    return held


def first_halves(grads):
    lead, rows_all, cols_all = grads[0].shape
    span = lax.axis_size("fsdp")
    pair = lax.axis_size("ctx")
    rows = rows_all // (span * pair)
    mine = lax.axis_index("ctx")
    cut = lambda g, which: lax.dynamic_index_in_dim(
        g.reshape(lead, span, pair, rows, cols_all), which, 2, keepdims=False
    )
    pick = lambda which: sum(cut(g, which) for g in grads)
    return pick(1 - mine).astype(BF16), pick(mine)


def joined(send, keep, axis, bit):
    return keep + swap(send, axis, bit).astype(F32)


def halves(total, axis, bit, used):
    mine = own_bit(axis, bit)
    if axis == "tp":
        half = total.shape[-1] // 2
        cut = lambda which: lax.dynamic_slice_in_dim(total, which * half, half, 3)
    else:
        lead, span, rows_here, cols_here = total.shape
        low = 1
        for other_bit in bits("fsdp"):
            if other_bit < bit and other_bit not in used:
                low *= 2
        view = total.reshape(lead, span // (2 * low), 2, low, rows_here, cols_here)
        cut = lambda which: lax.dynamic_index_in_dim(view, which, 2, keepdims=False).reshape(
            lead, span // 2, rows_here, cols_here
        )
    return cut(1 - mine).astype(BF16), cut(mine)


def scatter_steps(total, order, used):
    used = set(used)
    for axis, bit in order:
        total = joined(*halves(total, axis, bit, used), axis, bit)
        if axis == "fsdp":
            used.add(bit)
    return total


def layer_stats(values_in):
    mean_row = jnp.mean(values_in, axis=-1, keepdims=True)
    centered = values_in - mean_row
    inverse = lax.rsqrt(jnp.mean(centered * centered, axis=-1, keepdims=True) + EPSILON)
    return (centered * inverse, inverse)


def layer_back(grad_out, normed, inverse, gain_row):
    scaled = grad_out * gain_row
    return inverse * (
        scaled
        - jnp.mean(scaled, axis=-1, keepdims=True)
        - normed * jnp.mean(scaled * normed, axis=-1, keepdims=True)
    )


def mm(left, right, left_dim, right_dim):
    return lax.dot_general(
        left, right, (((left_dim,), (right_dim,)), ((), ())), preferred_element_type=F32
    )


def head_select():
    row = lax.broadcasted_iota(jnp.int32, (TALL, LANES), 0) // AREA
    lane = lax.broadcasted_iota(jnp.int32, (TALL, LANES), 1) // HEAD_DIM
    return (row == lane).astype(F32)


def spread(value, select):
    return jnp.concatenate([value] * GROUP, axis=0) * select


def fold(tall, select):
    return jnp.sum((tall * select).reshape(GROUP, AREA, LANES), axis=0)


def forward_kernel(
    x_ref, vec_ref, w_ref, bias_ref, mask_ref, *rest
):
    tok_ref, q_ref, k_ref, v_ref, p_ref, att_ref, mid_ref, n2_ref = rest[-8:]
    vec = vec_ref[...]
    resid = x_ref[...]
    norm, _ = layer_stats(resid)
    tok = (norm * vec[0:1] + vec[2:3]).astype(BF16)
    tok_ref[...] = tok
    q_ref[...] = (mm(tok, w_ref[0], 1, 0) + vec[6:7]).astype(BF16)
    k_ref[...] = mm(tok, w_ref[1], 1, 0).astype(BF16)
    v_ref[...] = (mm(tok, w_ref[2], 1, 0) + vec[7:8]).astype(BF16)
    select = head_select()
    select_half = select.astype(BF16)

    def window(w, carry):
        here = pl.ds(pl.multiple_of(w * AREA, AREA), AREA)
        mask = mask_ref[w]
        mask_tall = jnp.concatenate([mask] * GROUP, axis=0)
        for g in range(w_ref.shape[2] // LANES):
            part = slice(g * LANES, (g + 1) * LANES)
            tall_q = spread(q_ref[here, part], select_half)
            scores = mm(tall_q, k_ref[here, part], 1, 1) * SCALE
            scores = scores + bias_ref[g * TALL : (g + 1) * TALL, :] + mask_tall
            peak = jnp.max(scores, axis=-1, keepdims=True)
            weight = jnp.exp(scores - peak)
            prob = weight / jnp.sum(weight, axis=-1, keepdims=True)
            p_ref[w, g] = prob
            att_ref[here, part] = fold(
                mm(prob.astype(BF16), v_ref[here, part], 1, 0), select
            ).astype(BF16)
        return carry

    lax.fori_loop(0, PER_STEP, window, 0, unroll=True)
    middle = resid + mm(att_ref[...], w_ref[3], 1, 1) + vec[4:5]
    mid_ref[...] = middle
    norm_two, _ = layer_stats(middle)
    n2_ref[...] = (norm_two * vec[1:2] + vec[3:4]).astype(BF16)


def ffn_kernel(
    mid_ref, n2_ref, cot_ref, up_ref, down_ref, upb_ref, vec_ref,
    out_ref, gm_ref, dffn_ref, dupb_ref, sums_ref, acc_ref, g2_ref
):
    @pl.when(pl.program_id(0) == 0)
    def _():
        dffn_ref[...] = jnp.zeros_like(dffn_ref)
        dupb_ref[...] = jnp.zeros_like(dupb_ref)
        sums_ref[...] = jnp.zeros_like(sums_ref)

    vec = vec_ref[...]
    chunk = 512
    acc_ref[...] = jnp.zeros_like(acc_ref)
    g2_ref[...] = jnp.zeros_like(g2_ref)

    def step(f, carry):
        here = pl.ds(pl.multiple_of(f * chunk, chunk), chunk)
        rows_two = n2_ref[...]
        cot_half = cot_ref[...].astype(BF16)
        pre = mm(rows_two, up_ref[:, here], 1, 0) + upb_ref[:, here]
        phi = 0.5 * (1.0 + lax.erf(pre * (1.0 / math.sqrt(2.0))))
        hidden = (pre * phi).astype(BF16)
        slope = mm(cot_half, down_ref[:, here], 1, 0) * (
            phi + pre * jnp.exp(-0.5 * pre * pre) * (1.0 / math.sqrt(2.0 * math.pi))
        )
        slope_half = slope.astype(BF16)
        acc_ref[...] += mm(hidden, down_ref[:, here], 1, 1)
        g2_ref[...] += mm(slope_half, up_ref[:, here], 1, 1)
        dffn_ref[0, :, here] += mm(rows_two, slope_half, 0, 0)
        dffn_ref[1, :, here] += mm(cot_half, hidden, 0, 0)
        dupb_ref[:, here] += jnp.sum(slope, axis=0, keepdims=True)
        return carry

    lax.fori_loop(0, up_ref.shape[1] // chunk, step, 0, unroll=True)
    middle = mid_ref[...]
    cot = cot_ref[...]
    out_ref[...] = middle + acc_ref[...] + vec[5:6]
    norm_two, inv_two = layer_stats(middle)
    grad_two = g2_ref[...]
    grad_mid = cot + layer_back(grad_two, norm_two, inv_two, vec[1:2])
    gm_ref[...] = grad_mid
    total = lambda value: jnp.sum(value, axis=0, keepdims=True)
    sums_ref[0:1] += total(grad_two * norm_two)
    sums_ref[1:2] += total(grad_two)
    sums_ref[2:3] += total(grad_mid)
    sums_ref[3:4] += total(cot)


def backward_kernel(
    x_ref, gm_ref, tok_ref, q_ref, k_ref, v_ref, p_ref, att_ref, w_ref, vec_ref, *rest
):
    img_ref, dw_ref, ds_ref, sums_ref, ga_ref, mixed_ref = rest[-6:]

    @pl.when(pl.program_id(0) == 0)
    def _():
        dw_ref[...] = jnp.zeros_like(dw_ref)
        ds_ref[...] = jnp.zeros_like(ds_ref)
        sums_ref[...] = jnp.zeros_like(sums_ref)

    vec = vec_ref[...]
    grad_mid = gm_ref[...]
    grad_tok = grad_mid.astype(BF16)
    ga_ref[...] = mm(grad_tok, w_ref[3], 1, 0).astype(BF16)
    dw_ref[3] += mm(grad_tok, att_ref[...], 0, 0)
    select = head_select()
    select_half = select.astype(BF16)
    total = lambda value: jnp.sum(value, axis=0, keepdims=True)

    def window(w, carry):
        here = pl.ds(pl.multiple_of(w * AREA, AREA), AREA)
        for g in range(w_ref.shape[2] // LANES):
            part = slice(g * LANES, (g + 1) * LANES)
            tall_q = spread(q_ref[here, part], select_half)
            tall_ga = spread(ga_ref[here, part], select_half)
            prob = p_ref[w, g]
            grad_prob = mm(tall_ga, v_ref[here, part], 1, 1)
            grad_value = mm(prob.astype(BF16), tall_ga, 0, 0)
            weighted = prob * grad_prob
            grad_score = weighted - prob * jnp.sum(weighted, axis=-1, keepdims=True)
            ds_ref[g * TALL : (g + 1) * TALL, :] += grad_score
            score_half = (grad_score * SCALE).astype(BF16)
            grad_query = fold(mm(score_half, k_ref[here, part], 1, 0), select)
            grad_key = mm(score_half, tall_q, 0, 0)
            sums_ref[0:1, part] += total(grad_query)
            sums_ref[1:2, part] += total(grad_value)
            mixed_ref[0, here, part] = grad_query.astype(BF16)
            mixed_ref[1, here, part] = grad_key.astype(BF16)
            mixed_ref[2, here, part] = grad_value.astype(BF16)
        return carry

    lax.fori_loop(0, PER_STEP, window, 0, unroll=True)
    tok = tok_ref[...]
    grad_one = jnp.zeros(grad_mid.shape, F32)
    for j in range(3):
        dw_ref[j] += mm(tok, mixed_ref[j], 0, 0)
        grad_one = grad_one + mm(mixed_ref[j], w_ref[j], 1, 1)
    norm, inv = layer_stats(x_ref[...])
    img_ref[...] = grad_mid + layer_back(grad_one, norm, inv, vec[0:1])
    sums_ref[2:3] += total(grad_one * norm)
    sums_ref[3:4] += total(grad_one)


def to_padded(field):
    images, rows, cols = field.shape[:3]
    rest = field.shape[3:]
    cut = field.reshape(images, rows // WIN, WIN, cols // WIN, WIN, *rest)
    grow = PAD - WIN
    cut = jnp.pad(cut, ((0, 0), (0, 0), (0, grow), (0, 0), (0, grow)) + ((0, 0),) * len(rest))
    order = (0, 1, 3, 2, 4) + tuple(range(5, 5 + len(rest)))
    return cut.transpose(order).reshape(-1, *rest)


def from_padded(tiles, images, rows, cols):
    width = tiles.shape[-1]
    cut = tiles.reshape(images, rows // WIN, cols // WIN, PAD, PAD, width)
    cut = cut.transpose(0, 1, 3, 2, 4, 5)[:, :, :WIN, :, :WIN]
    return cut.reshape(images, rows, cols, width)


def whole_spec(shape):
    return pl.BlockSpec(shape, lambda i: (0,) * len(shape))


def row_spec(cols, first=0):
    return pl.BlockSpec((ROWS, cols), lambda i: (i + first, 0))


PARAMS = dict(compiler_params=pltpu.CompilerParams(vmem_limit_bytes=60 * 1024 * 1024))


def per_device(
    image, cotangent, norm_gain, norm_bias, qkv_weight, qkv_bias, bias_table, bias_index,
    regions, proj_weight, out_bias, up_weight, up_bias, down_weight,
):
    images, band_rows, columns, channels = image.shape
    groups = lax.axis_size("tp")
    table_rows = bias_table.shape[1]
    head_width = qkv_weight.shape[2]
    heads_here = bias_table.shape[0]
    ffn_here = up_bias.shape[0]
    rows_here = qkv_weight.shape[0]

    shards = lax.axis_size("fsdp") * lax.axis_size("ctx")
    small_parts = [
        norm_gain.reshape(-1), norm_bias.reshape(-1), out_bias.reshape(-1), qkv_bias.reshape(-1),
        up_bias, bias_table.reshape(-1),
    ]
    small_len = sum(part.shape[0] for part in small_parts)
    small_rows = -(-small_len // (16 * head_width)) * 16
    small_parts.append(jnp.zeros((small_rows * head_width - small_len,), BF16))
    attn_block = jnp.concatenate(
        [
            qkv_weight[:, 0], qkv_weight[:, 1], qkv_weight[:, 2], proj_weight.T,
            jnp.concatenate(small_parts).reshape(small_rows, head_width),
        ],
        axis=0,
    )
    ffn_block = jnp.stack([up_weight, down_weight.T])
    far, near = split_bits()
    across = [("tp", bit) for bit in bits("tp")]
    last = [("ctx", bit) for bit in bits("ctx")[::-1]]
    attn_all = gather_steps(attn_block, far + near + across + last)
    attn_all = attn_all.reshape(shards, 4 * rows_here + small_rows, groups * head_width)
    attn_w = (
        attn_all[:, : 4 * rows_here]
        .reshape(shards, 4, rows_here, channels)
        .transpose(1, 0, 2, 3)
        .reshape(4, channels, channels)
    )
    ffn_far = gather_steps(ffn_block, far)
    up_held = gather_steps(ffn_far[0], across)
    down_held = gather_steps(ffn_far[1], near)
    up_held, down_held, attn_w = lax.optimization_barrier((up_held, down_held, attn_w))
    up_held = gather_steps(up_held, near)
    down_held = gather_steps(down_held, across)

    small = (
        attn_all[:, 4 * rows_here :]
        .reshape(shards, small_rows, groups, head_width)
        .transpose(0, 2, 1, 3)
        .reshape(shards, groups, -1)
    )
    v_end = 6 * rows_here
    vec_six = (
        small[:, 0, :v_end].reshape(shards, 6, rows_here).transpose(1, 0, 2).reshape(6, channels)
    ).astype(F32)
    small = small[0, :, v_end:small_len]
    qb_end = 2 * head_width
    pair_whole = (
        small[:, :qb_end].reshape(groups, 2, head_width).transpose(1, 0, 2).reshape(2, -1).astype(F32)
    )
    upb_whole = small[:, qb_end : qb_end + ffn_here].reshape(1, -1).astype(F32)
    table_whole = small[:, qb_end + ffn_here :].reshape(groups * heads_here, table_rows)
    vec = jnp.concatenate([vec_six, pair_whole], axis=0)

    edge_image, edge_grad = shifted((image[:, :SHIFT], cotangent[:, :SHIFT]), "ctx", -1)
    residual = jnp.concatenate([image[:, SHIFT:], edge_image], axis=1)
    grad_top = jnp.concatenate([cotangent[:, SHIFT:], edge_grad], axis=1)
    edge_image, edge_grad = shifted((residual[:, :, :SHIFT], grad_top[:, :, :SHIFT]), "tp", -1)
    residual = to_padded(jnp.concatenate([residual[:, :, SHIFT:], edge_image], axis=2))
    grad_top = to_padded(jnp.concatenate([grad_top[:, :, SHIFT:], edge_grad], axis=2))
    tokens_all = residual.shape[0]
    windows = tokens_all // AREA

    grow = PAD - WIN
    index_pad = jnp.pad(
        bias_index.reshape(WIN, WIN, WIN, WIN), ((0, grow),) * 4, constant_values=-1
    ).reshape(-1)
    one_hot = index_pad[:, None] == jnp.arange(table_rows, dtype=jnp.int32)
    heads_all = table_whole.shape[0]
    rel_bias = jnp.einsum(
        "ht,qt->hq", table_whole, one_hot.astype(BF16), preferred_element_type=F32
    ).reshape(heads_all * AREA, AREA)
    key_spot = jnp.arange(AREA, dtype=jnp.int32)
    key_live = (key_spot // PAD < WIN) & (key_spot % PAD < WIN)
    rel_bias = jnp.where(key_live[None, :], rel_bias, ABSENT)
    col_start = lax.axis_index("tp") * columns
    region_here = lax.dynamic_slice_in_dim(regions, col_start, columns, 1)
    labels = to_padded(region_here[None]).reshape(windows // images, AREA)
    labels = jnp.concatenate([labels] * images, axis=0)
    mask_bias = jnp.where(labels[:, :, None] == labels[:, None, :], 0.0, MASKED).astype(F32)

    steps = tokens_all // ROWS
    sets = heads_all // GROUP
    half_steps = [steps] if steps < 2 else [steps // 2, steps - steps // 2]
    rows_full = jax.ShapeDtypeStruct((tokens_all, channels), F32)
    rows_all_half = jax.ShapeDtypeStruct((tokens_all, channels), BF16)
    prob_spec = pl.BlockSpec((PER_STEP, sets, TALL, AREA), lambda i: (i, 0, 0, 0))
    row = row_spec(channels)
    anywhere = pl.BlockSpec(memory_space=pl.ANY)
    dense = 2 * ROWS * channels * channels
    moved = ROWS * channels

    saved = []
    carried = ()
    for part, count in enumerate(half_steps):
        first = part * half_steps[0]
        placed = row_spec(channels, first)
        rows_half = jax.ShapeDtypeStruct((count * ROWS, channels), BF16)
        prob_shape = jax.ShapeDtypeStruct((count * PER_STEP, sets, TALL, AREA), F32)
        mask_spec = pl.BlockSpec((PER_STEP, AREA, AREA), lambda i, first=first: (i + first, 0, 0))
        mask_here = mask_bias
        if part:
            up_held, down_held, mask_here = lax.optimization_barrier((up_held, down_held, mask_bias))
        *kept, middle, normed_two = pl.pallas_call(
            forward_kernel,
            grid=(count,),
            in_specs=[
                placed, whole_spec(vec.shape), whole_spec(attn_w.shape), whole_spec(rel_bias.shape),
                mask_spec,
            ]
            + [anywhere] * len(carried),
            out_specs=[row, row, row, row, prob_spec, row, placed, placed],
            out_shape=[rows_half] * 4 + [prob_shape, rows_half, rows_full, rows_all_half],
            input_output_aliases={5 + n: 6 + n for n in range(len(carried))},
            cost_estimate=pl.CostEstimate(
                flops=40 * count * dense, bytes_accessed=20 * count * moved, transcendentals=0
            ),
            **PARAMS,
        )(residual, vec, attn_w, rel_bias, mask_here, *carried)
        carried = (middle, normed_two)
        saved.append(kept)

    up_w = gather_steps(up_held, last).reshape(channels, -1)
    down_w = gather_steps(down_held, last).reshape(channels, -1)
    ffn_all = up_w.shape[1]
    output_full, grad_mid, dffn, dupb, sums_two = pl.pallas_call(
        ffn_kernel,
        grid=(steps,),
        in_specs=[
            row, row, row, whole_spec(up_w.shape), whole_spec(down_w.shape),
            whole_spec(upb_whole.shape), whole_spec(vec.shape),
        ],
        out_specs=[
            row, row, whole_spec((2,) + up_w.shape), whole_spec((1, ffn_all)),
            whole_spec((8, channels)),
        ],
        out_shape=[
            rows_full, rows_full, jax.ShapeDtypeStruct((2,) + up_w.shape, F32), jax.ShapeDtypeStruct((1, ffn_all), F32),
            jax.ShapeDtypeStruct((8, channels), F32),
        ],
        scratch_shapes=[pltpu.VMEM((ROWS, channels), F32), pltpu.VMEM((ROWS, channels), F32)],
        cost_estimate=pl.CostEstimate(
            flops=60 * steps * dense, bytes_accessed=40 * steps * moved, transcendentals=0
        ),
        **PARAMS,
    )(middle, normed_two, grad_top, up_w, down_w, upb_whole, vec)
    across_high = across[::-1]
    ffn_total = joined(*first_halves([dffn]), "ctx", 1)
    orders = (across_high + near, near + across_high)

    weight_parts, score_parts, sum_parts = [], [], []
    carried = ()
    for part, count in enumerate(half_steps):
        first = part * half_steps[0]
        placed = row_spec(channels, first)
        gm_here = grad_mid
        if part:
            up_cut = halves(ffn_total[:1], *orders[0][0], ())
            down_cut = halves(ffn_total[1:], *orders[1][0], ())
            up_cut, down_cut, gm_here = lax.optimization_barrier((up_cut, down_cut, grad_mid))
            up_total = joined(*up_cut, *orders[0][0])
            down_total = joined(*down_cut, *orders[1][0])
            orders = (orders[0][1:], orders[1][1:])
        grad_full, dw, grad_score, sums_one = pl.pallas_call(
            backward_kernel,
            grid=(count,),
            in_specs=[
                placed, placed, row, row, row, row, prob_spec, row, whole_spec(attn_w.shape),
                whole_spec(vec.shape),
            ]
            + [anywhere] * len(carried),
            out_specs=[
                placed, whole_spec(attn_w.shape), whole_spec(rel_bias.shape),
                whole_spec((8, channels)),
            ],
            out_shape=[
                rows_full, jax.ShapeDtypeStruct(attn_w.shape, F32),
                jax.ShapeDtypeStruct(rel_bias.shape, F32),
                jax.ShapeDtypeStruct((8, channels), F32),
            ],
            input_output_aliases={10 + n: n for n in range(len(carried))},
            scratch_shapes=[
                pltpu.VMEM((ROWS, channels), BF16), pltpu.VMEM((3, ROWS, channels), BF16)
            ],
            cost_estimate=pl.CostEstimate(
                flops=60 * count * dense, bytes_accessed=40 * count * moved, transcendentals=0
            ),
            **PARAMS,
        )(residual, gm_here, *saved[part], attn_w, vec, *carried)
        carried = (grad_full,)
        weight_parts.append(dw)
        score_parts.append(grad_score)
        sum_parts.append(sums_one)
    if len(half_steps) == 1:
        up_total, down_total = ffn_total[:1], ffn_total[1:]
    else:
        up_total, down_total, weight_parts, score_parts, sum_parts, grad_full = (
            lax.optimization_barrier(
                (up_total, down_total, weight_parts, score_parts, sum_parts, grad_full)
            )
        )
    sums_one = sum(sum_parts)
    table_all = jnp.einsum(
        "hq,qt->ht",
        sum(score_parts).reshape(heads_all, AREA * AREA),
        one_hot.astype(F32),
        precision=lax.Precision.HIGHEST,
    )
    small_total = jnp.concatenate(
        [
            sums_one[:4].reshape(-1), sums_two[:4].reshape(-1), dupb.reshape(-1),
            table_all.reshape(-1),
        ]
    )
    small_plan = [(axis, bit) for axis in ("ctx", "tp", "fsdp") for bit in bits(axis)]
    attn_plan = [("ctx", 1)] + near + across_high + far
    up_plan, down_plan, ffn_plan = list(orders[0]), list(orders[1]), list(far)
    up_used = {bit for axis, bit in near if (axis, bit) not in up_plan}
    down_used = {bit for axis, bit in near if (axis, bit) not in down_plan}
    ffn_used = {bit for _, bit in near}
    attn_used = set()
    attn_sums, ffn_sums = None, None
    while attn_plan or small_plan or up_plan or down_plan or ffn_plan:
        if attn_plan:
            move = attn_plan.pop(0)
            if attn_sums is None:
                attn_sums = joined(*first_halves(weight_parts), *move)
            else:
                attn_sums = scatter_steps(attn_sums, [move], attn_used)
                attn_used |= {move[1]} if move[0] == "fsdp" else set()
        if small_plan:
            axis, bit = small_plan.pop(0)
            small_total = small_total + swap(small_total, axis, bit)
        if up_plan or down_plan:
            if up_plan:
                move = up_plan.pop(0)
                up_total = scatter_steps(up_total, [move], up_used)
                up_used |= {move[1]} if move[0] == "fsdp" else set()
            if down_plan:
                move = down_plan.pop(0)
                down_total = scatter_steps(down_total, [move], down_used)
                down_used |= {move[1]} if move[0] == "fsdp" else set()
            up_total, down_total, attn_sums, small_total = lax.optimization_barrier(
                (up_total, down_total, attn_sums, small_total)
            )
        else:
            if ffn_sums is None:
                ffn_sums = jnp.concatenate([up_total, down_total], axis=0)
            if ffn_plan:
                move = ffn_plan.pop(0)
                ffn_sums = scatter_steps(ffn_sums, [move], ffn_used)
                ffn_used.add(move[1])
            ffn_sums, attn_sums, small_total = lax.optimization_barrier(
                (ffn_sums, attn_sums, small_total)
            )
    if ffn_sums is None:
        ffn_sums = jnp.concatenate([up_total, down_total], axis=0)
    ffn_sums, attn_sums = ffn_sums[:, 0], attn_sums[:, 0]
    cut = 4 * channels
    one_sum = small_total[:cut].reshape(4, channels)
    two_sum = small_total[cut : 2 * cut].reshape(4, channels)
    upb_sum = small_total[2 * cut : 2 * cut + ffn_all]
    table_sum = small_total[2 * cut + ffn_all :].reshape(heads_all, table_rows)
    tp_index = lax.axis_index("tp")
    shard = lax.axis_index("fsdp") * lax.axis_size("ctx") + lax.axis_index("ctx")
    take = lambda value: lax.dynamic_slice_in_dim(value, shard * rows_here, rows_here, 1)
    gain_grad = take(jnp.stack([one_sum[2], two_sum[0]]))
    bias_grad = take(jnp.stack([one_sum[3], two_sum[1]]))
    out_grad = take(jnp.stack([two_sum[2], two_sum[3]]))
    qkv_bias_grad = lax.dynamic_slice_in_dim(one_sum[:2], tp_index * head_width, head_width, 1)
    up_bias_grad = lax.dynamic_slice_in_dim(upb_sum, tp_index * ffn_here, ffn_here, 0)
    table_grad = lax.dynamic_slice_in_dim(table_sum, tp_index * heads_here, heads_here, 0)

    output_full = from_padded(output_full, images, band_rows, columns)
    grad_full = from_padded(grad_full, images, band_rows, columns)
    edge_out, edge_back = shifted((output_full[:, :, -SHIFT:], grad_full[:, :, -SHIFT:]), "tp", 1)
    output_shift = jnp.concatenate([edge_out, output_full[:, :, :-SHIFT]], axis=2)
    grad_start = jnp.concatenate([edge_back, grad_full[:, :, :-SHIFT]], axis=2)
    edge_out, edge_back = shifted((output_shift[:, -SHIFT:], grad_start[:, -SHIFT:]), "ctx", 1)
    output = jnp.concatenate([edge_out, output_shift[:, :-SHIFT]], axis=1)
    image_grad = jnp.concatenate([edge_back, grad_start[:, :-SHIFT]], axis=1)
    return (
        output, image_grad, gain_grad, bias_grad,
        jnp.stack([attn_sums[0], attn_sums[1], attn_sums[2]], axis=1),
        qkv_bias_grad, table_grad, attn_sums[3].T, out_grad, ffn_sums[0], up_bias_grad,
        ffn_sums[1].T,
    )


def solution(mesh):
    in_specs = (
        P("fsdp", "ctx", "tp", None),
        P("fsdp", "ctx", "tp", None),
        P(None, ("fsdp", "ctx")),
        P(None, ("fsdp", "ctx")),
        P(("fsdp", "ctx"), None, "tp"),
        P(None, "tp"),
        P("tp", None),
        P(),
        P("ctx", None),
        P("tp", ("fsdp", "ctx")),
        P(None, ("fsdp", "ctx")),
        P(("fsdp", "ctx"), "tp"),
        P("tp"),
        P("tp", ("fsdp", "ctx")),
    )
    out_specs = (
        P("fsdp", "ctx", "tp", None),
        P("fsdp", "ctx", "tp", None),
        P(None, ("fsdp", "ctx")),
        P(None, ("fsdp", "ctx")),
        P(("fsdp", "ctx"), None, "tp"),
        P(None, "tp"),
        P("tp", None),
        P("tp", ("fsdp", "ctx")),
        P(None, ("fsdp", "ctx")),
        P(("fsdp", "ctx"), "tp"),
        P("tp"),
        P("tp", ("fsdp", "ctx")),
    )
    return jax.shard_map(
        per_device, mesh=mesh, in_specs=in_specs, out_specs=out_specs, check_vma=False
    )
```
